512 devices in a mesh: row: 64 (over x, z, core), col: 8 (over y).
Axes of the slice: x: 4, y: 8, z: 8, core: 2. Of those that a mesh axis runs over, the one named last changes fastest.
Arguments:
- source: bfloat16 [16384, 64], P('row'), may hold values from -4 to 4
- target: bfloat16 [4096, 64], P('col'), may hold values from -4 to 4
- log_source: float32 [16384], P('row'), may hold values from -1.5 to 1.5
- log_target: float32 [4096], P('col'), may hold values from -1.5 to 1.5
Outputs:
- source_map: float32 [16384, 64], P('row')
- target_map: float32 [4096, 64], P('col')
The draws below stay inside these ranges and needn't reach their ends.
All inputs are finite; a program needn't handle non-finite values.
Results may differ from the reference program's by a relative error of at most 0.0025.
Values sent between devices are 32-bit elements; how exact they have to be, the bound alone decides.
A program may use at most 128 MiB of HBM per device.

```python
import jax
import jax.numpy as jnp
from jax import lax

DIM = 64
S_DEV = 256
ITERS = 4
SOURCES = 16384
TARGETS = 4096
N_ROW = 64


def normal_points(key, row_count, limit):
    return jnp.clip(jax.random.normal(key, (row_count, DIM), jnp.float32), -limit, limit)


def draw_source(key, part):
    key = jax.random.fold_in(key, 11)
    values = normal_points(key, SOURCES, 4.0)
    return values.astype(jnp.bfloat16)


def draw_target(key, part):
    key = jax.random.fold_in(key, 23)
    values = normal_points(key, TARGETS, 4.0)
    return values.astype(jnp.bfloat16)


def steps_of(stream_key, extent, shards, smallest, high):
    def one(axis_at, parts):
        steps = jax.random.uniform(jax.random.fold_in(jax.random.fold_in(stream_key, 6), axis_at), (parts,), jnp.float32, smallest / len(shards), high / len(shards))
        return jnp.repeat(jnp.exp(steps), extent[axis_at] // parts).reshape((-1,) + (1,) * (len(extent) - axis_at - 1))

    loudness = one(*shards[0])
    for cut in shards[1:]:
        loudness = loudness * one(*cut)
    return loudness


def setup_inputs(seed: int = 0) -> dict:
    key_list = jax.random.split(jax.random.key(seed), 5)
    return {
        "source": draw_source(jax.random.fold_in(key_list[4], 71), 0),
        "target": draw_target(jax.random.fold_in(key_list[4], 71), 0),
        "log_source": jnp.clip(jax.random.uniform(key_list[2], (SOURCES,), jnp.float32, -1.5, 1.5) * steps_of(key_list[2], (SOURCES,), ((0, 64),), -0.4, 0.0), -1.5, 1.5),
        "log_target": jnp.clip(jax.random.uniform(key_list[3], (TARGETS,), jnp.float32, -1.5, 1.5) * steps_of(key_list[3], (TARGETS,), ((0, 8),), -0.4, 0.0), -1.5, 1.5),
    }


entropy_weight = 3.0


def cost_rows(source_rows, rows_norm, target, target_norm):
    inner = jnp.dot(source_rows, target.T, preferred_element_type=jnp.float32)
    return rows_norm[:, None] + target_norm[None, :] - 2.0 * inner


def reference(source, target, log_source, log_target):
    source_norm = jnp.sum(jnp.square(source.astype(jnp.float32)), axis=1)
    target_norm = jnp.sum(jnp.square(target.astype(jnp.float32)), axis=1)
    source_blocks = source.reshape(N_ROW, S_DEV, DIM)
    norm_blocks = source_norm.reshape(N_ROW, S_DEV)
    mass_blocks = log_source.reshape(N_ROW, S_DEV)

    def row_update(col_scaling):
        def per_block(portion):
            rows_here, norms, masses = portion
            scores = (col_scaling[None, :] - cost_rows(rows_here, norms, target, target_norm)) / entropy_weight
            highest = jnp.max(scores, axis=1)
            summed = jnp.sum(jnp.exp(scores - highest[:, None]), axis=1)
            return entropy_weight * masses - entropy_weight * (highest + jnp.log(summed))
        return lax.map(per_block, (source_blocks, norm_blocks, mass_blocks)).reshape(SOURCES)

    def col_update(row_scaling):
        scaling_blocks = row_scaling.reshape(N_ROW, S_DEV)

        def accumulate(carried, portion):
            rows_here, norms, scaling = portion
            scores = (scaling[:, None] - cost_rows(rows_here, norms, target, target_norm)) / entropy_weight
            highest = jnp.maximum(carried[0], jnp.max(scores, axis=0))
            summed = carried[1] * jnp.exp(carried[0] - highest) + jnp.sum(jnp.exp(scores - highest[None, :]), axis=0)
            return (highest, summed), None

        initial = (jnp.full((TARGETS,), -1e30, jnp.float32), jnp.zeros((TARGETS,), jnp.float32))
        (highest, summed), unused = lax.scan(accumulate, initial, (source_blocks, norm_blocks, scaling_blocks))
        return entropy_weight * log_target - entropy_weight * (highest + jnp.log(summed)), highest

    col_scaling = jnp.zeros((TARGETS,), jnp.float32)
    row_scaling = jnp.zeros((SOURCES,), jnp.float32)
    highest_col = jnp.zeros((TARGETS,), jnp.float32)
    for iteration in range(ITERS):
        row_scaling = row_update(col_scaling)
        col_scaling, highest_col = col_update(row_scaling)

    def source_block(portion):
        rows_here, norms = portion
        scores = (col_scaling[None, :] - cost_rows(rows_here, norms, target, target_norm)) / entropy_weight
        highest = jnp.max(scores, axis=1)
        weights = jnp.exp(scores - highest[:, None]).astype(jnp.bfloat16)
        denominator = jnp.sum(weights.astype(jnp.float32), axis=1)
        numerator = jnp.dot(weights, target, preferred_element_type=jnp.float32)
        return numerator / denominator[:, None]

    source_map = lax.map(source_block, (source_blocks, norm_blocks)).reshape(SOURCES, DIM)

    scaling_blocks = row_scaling.reshape(N_ROW, S_DEV)

    def target_accumulate(carried, portion):
        rows_here, norms, scaling = portion
        scores = (scaling[:, None] - cost_rows(rows_here, norms, target, target_norm)) / entropy_weight
        weights = jnp.exp(scores - highest_col[None, :]).astype(jnp.bfloat16)
        denominator = carried[0] + jnp.sum(weights.astype(jnp.float32), axis=0)
        numerator = carried[1] + jnp.dot(weights.T, rows_here, preferred_element_type=jnp.float32)
        return (denominator, numerator), None

    initial = (jnp.zeros((TARGETS,), jnp.float32), jnp.zeros((TARGETS, DIM), jnp.float32))
    (denominator, numerator), unused = lax.scan(target_accumulate, initial, (source_blocks, norm_blocks, scaling_blocks))
    target_map = numerator / denominator[:, None]
    return source_map, target_map
```

```python
import functools

import jax
import jax.numpy as jnp
from jax import lax
from jax.experimental import pallas as pl
from jax.experimental.pallas import tpu as pltpu
from jax.sharding import PartitionSpec as P

ITERS = 4
EPS = 3.0
LOG2E = 1.4426950408889634
SCALE = LOG2E / EPS
SHIFT = 40.0

NX, NZ, NC, NY = 4, 8, 2, 8
NG = NX * NC
S, T, D = 256, 512, 64
BLK = 64
NB = T // BLK
F32, BF16 = jnp.float32, jnp.bfloat16
MESH = pl.DeviceIdType.MESH
RING8 = (4, 3, 5, 2, 6, 1, 7)
PLANE = tuple((dx, dc) for dx in (2, 1, 3) for dc in (1, 0)) + ((0, 1),)

PHASES = ("y1", "y2", "y3", "y4", "yg", "p1", "p2", "p3", "p4", "z1", "den", "num", "map", "src", "fa", "tgt", "fwd")
IDX = {name: i for i, name in enumerate(PHASES)}


def iota(shape, dim):
    return lax.broadcasted_iota(jnp.int32, shape, dim)


def lse2(slots):
    highest = jnp.max(slots, axis=0)
    return highest + jnp.log2(jnp.sum(jnp.exp2(slots - highest[None]), axis=0))


def nt(a, b):
    return lax.dot_general(a, b, (((1,), (1,)), ((), ())), preferred_element_type=F32)


def nn(a, b):
    return lax.dot_general(a, b, (((1,), (0,)), ((), ())), preferred_element_type=F32)


def pack(column, first):
    groups = column.reshape(BLK // 8, 8, 1)
    shape = (BLK // 8, 8, 128)
    return jnp.sum(jnp.where(iota(shape, 2) == iota(shape, 0) + first, groups, 0.0), axis=0)


def unpack(packed, first):
    shape = (BLK // 8, 8, 128)
    picked = jnp.where(iota(shape, 2) == iota(shape, 0) + first, packed[None], 0.0)
    return jnp.sum(picked, axis=2, keepdims=True).reshape(BLK, 1)


def as_column(row):
    parts = []
    for h in range(S // 128):
        part = row[:, h * 128 : (h + 1) * 128]
        diagonal = iota((128, 128), 0) == iota((128, 128), 1)
        parts.append(jnp.sum(jnp.where(diagonal, part, 0.0), axis=1, keepdims=True))
    return jnp.concatenate(parts, axis=0)


def kernel(
    src_ref, tgt_ref, ls_ref, lt_ref, out_s, out_t,
    y1, y2, y3, y4, yg, p1, p2, p3, p4, z1, den, num, mapped, src_all, fa, tgt_all,
    numt, mt_own, k_ref, mf, wb, ste, vcol, ssem, rsem,
):
    row, y = lax.axis_index("row"), lax.axis_index("col")
    x, z, c = row // (NZ * NC), lax.rem(row // NC, NZ), lax.rem(row, NC)
    g = x * NC + c

    def place(px, pz, pc, py):
        return ((px * NZ + pz) * NC + pc, py)

    y_peers = [place(x, z, c, lax.rem(y + d, NY)) for d in RING8]
    z_peers = [place(x, lax.rem(z + d, NZ), c, y) for d in RING8]
    g_pos = [(lax.rem(x + dx, NX), lax.rem(c + dc, NC)) for dx, dc in PLANE]
    g_peers = [place(px, z, pc, y) for px, pc in g_pos]
    g_index = [px * NC + pc for px, pc in g_pos]

    barrier = pltpu.get_barrier_semaphore()
    for peer in y_peers + z_peers + g_peers:
        pl.semaphore_signal(barrier, inc=1, device_id=peer, device_id_type=MESH)

    def send(name, source, target, peer):
        i = IDX[name]
        pltpu.make_async_remote_copy(
            src_ref=source, dst_ref=target, send_sem=ssem.at[i], recv_sem=rsem.at[i],
            device_id=peer, device_id_type=MESH,
        ).start()

    def share(name, buf, me, peers, value=None):
        if value is not None:
            buf[me] = value
        for peer in peers:
            send(name, buf.at[me], buf.at[me], peer)

    def landed(name, buf):
        span = buf.at[pl.ds(0, 7)]
        pltpu.make_async_copy(span, span, rsem.at[IDX[name]]).wait()

    def sent(name, buf):
        span = buf.at[pl.ds(0, 7)]
        pltpu.make_async_copy(span, span, ssem.at[IDX[name]]).wait()

    src, tgt = src_ref[...], tgt_ref[...]
    eye = (iota((D, D), 0) == iota((D, D), 1)).astype(BF16)
    src_t = nt(eye, src)
    src_norm = jnp.sum(src_t * src_t, axis=0, keepdims=True)
    tgt_f = tgt.astype(F32)
    tgt_norm = jnp.sum(tgt_f * tgt_f, axis=1, keepdims=True)
    scores = (src_norm + tgt_norm - 2.0 * nt(tgt, src)) * (-SCALE)
    mt_own[...] = scores
    highest = jnp.max(scores, axis=0, keepdims=True)
    partial = highest + jnp.log2(jnp.sum(jnp.exp2(scores - highest), axis=0, keepdims=True))
    src_all[z] = src_t
    tgt_t = nt(eye, tgt)
    tgt_all[0, y] = tgt_t[: D // 2]
    tgt_all[1, y] = tgt_t[D // 2 :]

    pl.semaphore_wait(barrier, 21)
    share("y1", y1, y, y_peers, partial)
    share("src", src_all, z, z_peers)
    for peer in y_peers:
        send("tgt", tgt_all.at[c, y], tgt_all.at[c, y], peer)

    log_a = ls_ref[...] * LOG2E
    lanes_of = (iota((8, T), 1) % 8 == iota((8, T), 0)).astype(F32)
    spread = (iota((T, 128), 0) // 8 == iota((T, 128), 1)).astype(F32)
    log_b = lax.dot_general(
        lt_ref[...] * LOG2E * lanes_of, spread, (((1,), (0,)), ((), ())),
        preferred_element_type=F32, precision=lax.Precision.HIGHEST,
    )
    mass_b = jnp.exp2(log_b)

    landed("y1", y1)
    f_own = log_a - lse2(y1[...])

    packed = jnp.zeros((8, 128), F32)
    for b in range(NB):
        s = mt_own[b * BLK : (b + 1) * BLK, :] + f_own
        highest = jnp.max(s, axis=1, keepdims=True)
        total = jnp.sum(jnp.exp2(s - highest), axis=1, keepdims=True)
        packed = packed + pack(highest + jnp.log2(total), b * (BLK // 8))
    share("p1", p1, g, g_peers, packed)
    share("fa", fa, z, z_peers, jnp.concatenate([f_own, log_a], axis=1))
    landed("p1", p1)
    share("z1", z1, z, z_peers, lse2(p1[...]))

    landed("fa", fa)
    landed("src", src_all)
    mass_a = jnp.exp2(fa[:, :, S:])
    ste[D:, :] = jnp.ones((D, NZ * S), BF16)

    def fill(zz, carry):
        block = src_all[zz]
        norm = jnp.sum(block * block, axis=0, keepdims=True)
        low = block.astype(BF16)
        inner = nn(tgt_ref[...], low)
        t32 = tgt_ref[...].astype(F32)
        tn = jnp.sum(t32 * t32, axis=1, keepdims=True)
        first = fa[zz][:, :S] + SHIFT
        k_ref[zz] = (norm + tn - 2.0 * inner) * (-SCALE) + first
        ste[pl.ds(0, D), pl.ds(pl.multiple_of(zz * S, S), S)] = low
        return carry

    lax.fori_loop(0, NZ, fill, 0)

    landed("z1", z1)
    g1 = log_b - lse2(z1[...])

    def rows_of(values):
        return jnp.sum(values, axis=1, keepdims=True)

    def build(b, acc):
        span = pl.ds(pl.multiple_of(b * BLK, BLK), BLK)
        block = jnp.exp2(k_ref[:, span, :] + unpack(g1, b * (BLK // 8))[None])
        k_ref[:, span, :] = block
        return acc + jnp.sum(block.reshape(NZ, BLK // 8, 8, S), axis=1)

    def row_pass(v):
        def body(b, acc):
            span = pl.ds(pl.multiple_of(b * BLK, BLK), BLK)
            block = k_ref[:, span, :] * unpack(v, b * (BLK // 8))[None]
            return acc + jnp.sum(block.reshape(NZ, BLK // 8, 8, S), axis=1)

        return lax.fori_loop(0, NB, body, jnp.zeros((NZ, 8, S), F32))

    def col_pass(u, keep=False):
        def body(b, acc):
            span = pl.ds(pl.multiple_of(b * BLK, BLK), BLK)
            block = k_ref[:, span, :] * u
            if keep:
                for zz in range(NZ):
                    wb[span, zz * S : (zz + 1) * S] = block[zz].astype(BF16)
            t = jnp.sum(block, axis=0)
            t = t[:, :128] + t[:, 128:]
            return acc + pack(jnp.sum(t, axis=1, keepdims=True), b * (BLK // 8))

        return lax.fori_loop(0, NB, body, jnp.zeros((8, 128), F32))

    def exchange_rows(name, buf, acc):
        share(name, buf, y, y_peers, rows_of(acc))

    def scaling_u(name, buf):
        landed(name, buf)
        return mass_a / jnp.sum(buf[...], axis=0)

    used = iota((8, 128), 1) < T // 8

    def scaling_v(name, buf):
        landed(name, buf)
        return jnp.where(used, mass_b / jnp.sum(buf[...], axis=0), 1.0)

    exchange_rows("y2", y2, lax.fori_loop(0, NB, build, jnp.zeros((NZ, 8, S), F32)))
    i = IDX["tgt"]
    span = tgt_all.at[0, pl.ds(0, 7)]
    pltpu.make_async_copy(span, span, rsem.at[i]).wait()
    sibling = place(x, z, 1 - c, y)
    for d in RING8:
        other = lax.rem(y + d, NY)
        send("fwd", tgt_all.at[c, other], tgt_all.at[c, other], sibling)
    u = scaling_u("y2", y2)
    share("p2", p2, g, g_peers, col_pass(u))
    i = IDX["fwd"]
    pltpu.make_async_copy(span, span, rsem.at[i]).wait()
    v = scaling_v("p2", p2)

    exchange_rows("y3", y3, row_pass(v))

    def full(yy, carry):
        block = jnp.concatenate([tgt_all[0, yy], tgt_all[1, yy]], axis=0)
        norm = jnp.sum(block * block, axis=0, keepdims=True)
        s32 = src_ref[...].astype(F32)
        sn = jnp.sum(s32 * s32, axis=1, keepdims=True)
        mf[yy] = (sn + norm - 2.0 * nn(src_ref[...], block.astype(BF16))) * (-SCALE)
        return carry

    lax.fori_loop(0, NY, full, 0)
    u = scaling_u("y3", y3)
    share("p3", p3, g, g_peers, col_pass(u))
    v = scaling_v("p3", p3)

    exchange_rows("y4", y4, row_pass(v))
    u = scaling_u("y4", y4)
    share("p4", p4, g, g_peers, col_pass(u, keep=True))
    weighted = nt(ste[...], wb[...])
    den[g] = weighted[D : D + 1]
    for n in range(NG):
        numt[n] = weighted[n * 8 : n * 8 + 8]
    num[g] = numt[g]
    for peer, index in zip(g_peers, g_index):
        send("den", den.at[g], den.at[g], peer)
        send("num", numt.at[index], num.at[g], peer)

    y4_own = jnp.sum(y4[:, z], axis=0)
    f_last = as_column(f_own + log_a - jnp.log2(y4_own) + SHIFT)

    def add_f(yy, carry):
        mf[yy] = mf[yy] + f_last
        return carry

    lax.fori_loop(0, NY, add_f, 0)
    g4 = g1 + jnp.log2(scaling_v("p4", p4))
    over = (iota((128, T), 0) == iota((128, T), 1) // 8).astype(F32)
    g4_rows = lax.dot_general(
        g4, over, (((1,), (0,)), ((), ())), preferred_element_type=F32, precision=lax.Precision.HIGHEST
    )
    g4_row = jnp.sum(g4_rows * lanes_of, axis=0, keepdims=True)
    share("yg", yg, y, y_peers, g4_row)

    landed("den", den)
    landed("num", num)
    share("map", mapped, g, g_peers, jnp.sum(num[...], axis=0) / jnp.sum(den[...], axis=0))

    landed("yg", yg)

    def finish(yy, acc):
        block = jnp.concatenate([tgt_all[0, yy], tgt_all[1, yy], jnp.ones((D, T), F32)], axis=0)
        weight = jnp.exp2(mf[yy] + yg[yy]).astype(BF16)
        return acc + nt(weight, block.astype(BF16))

    both = lax.fori_loop(0, NY, finish, jnp.zeros((S, 2 * D), F32))
    out_s[...] = both[:, :D] / both[:, D:]

    landed("map", mapped)
    for n in range(NG):
        out_t[n * 8 : n * 8 + 8, :] = mapped[n]

    for name, buf in (
        ("y1", y1), ("y2", y2), ("y3", y3), ("y4", y4), ("yg", yg), ("p1", p1), ("p2", p2), ("p3", p3), ("p4", p4),
        ("z1", z1), ("den", den), ("num", num), ("map", mapped), ("src", src_all), ("fa", fa),
        ("tgt", tgt_all.at[0]), ("fwd", tgt_all.at[0]),
    ):
        sent(name, buf)


def per_device(source, target, log_source, log_target):
    vmem = pl.BlockSpec(memory_space=pltpu.VMEM)
    n = len(PHASES)
    scratch = [
        pltpu.VMEM((NY, 1, S), F32),
        pltpu.VMEM((NY, NZ, 1, S), F32),
        pltpu.VMEM((NY, NZ, 1, S), F32),
        pltpu.VMEM((NY, NZ, 1, S), F32),
        pltpu.VMEM((NY, 1, T), F32),
        pltpu.VMEM((NG, 8, 128), F32),
        pltpu.VMEM((NG, 8, 128), F32),
        pltpu.VMEM((NG, 8, 128), F32),
        pltpu.VMEM((NG, 8, 128), F32),
        pltpu.VMEM((NZ, 8, 128), F32),
        pltpu.VMEM((NG, 1, T), F32),
        pltpu.VMEM((NG, 8, T), F32),
        pltpu.VMEM((NG, 8, T), F32),
        pltpu.VMEM((NZ, D, S), F32),
        pltpu.VMEM((NZ, 1, 2 * S), F32),
        pltpu.VMEM((2, NY, D // 2, T), F32),
        pltpu.VMEM((NG, 8, T), F32),
        pltpu.VMEM((T, S), F32),
        pltpu.VMEM((NZ, T, S), F32),
        pltpu.VMEM((NY, S, T), F32),
        pltpu.VMEM((T, NZ * S), BF16),
        pltpu.VMEM((2 * D, NZ * S), BF16),
        pltpu.VMEM((8, 128), F32),
        pltpu.SemaphoreType.DMA((n,)),
        pltpu.SemaphoreType.DMA((n,)),
    ]
    source_map, target_map = pl.pallas_call(
        kernel,
        out_shape=(jax.ShapeDtypeStruct((S, D), F32), jax.ShapeDtypeStruct((D, T), F32)),
        in_specs=[vmem] * 4,
        out_specs=(vmem, vmem),
        scratch_shapes=scratch,
        compiler_params=pltpu.CompilerParams(
            collective_id=0, has_side_effects=True, vmem_limit_bytes=48 * 1024 * 1024
        ),
    )(source, target, log_source.reshape(1, S), log_target.reshape(1, T))
    return source_map, target_map.T


def solution(mesh):
    in_specs = (P("row", None), P("col", None), P("row"), P("col"))
    out_specs = (P("row", None), P("col", None))
    return jax.shard_map(
        per_device, mesh=mesh, in_specs=in_specs, out_specs=out_specs, check_vma=False
    )
```

```python
import jax
import jax.numpy as jnp
from jax import lax
from jax.experimental import pallas as pl
from jax.experimental.pallas import tpu as pltpu
from jax.sharding import PartitionSpec as P

EPS = 3.0
LOG2E = 1.4426950408889634
SCALE = LOG2E / EPS
SHIFT = 40.0

NX, NZ, NC, NY = 4, 8, 2, 8
NG = NX * NC
ZH, YH = 4, 2
NR = NG * 2
FR = 64 // NR
S, T, D = 256, 512, 64
NK = T // 8
F32, BF16 = jnp.float32, jnp.bfloat16
MESH = pl.DeviceIdType.MESH
RING8 = (4, 3, 5, 2, 6, 1, 7)
PLANE = tuple((dx, dc) for dx in (2, 1, 3) for dc in (1, 0)) + ((0, 1),)

PHASES = (
    "y1", "y2", "y3", "y4", "yg", "p1", "z1", "p2", "p3", "p4", "den", "num", "map", "src", "fa", "ga", "tgt", "fwd",
)
IDX = {name: i for i, name in enumerate(PHASES)}


def iota(shape, dim):
    return lax.broadcasted_iota(jnp.int32, shape, dim)


def lse2(slots):
    highest = jnp.max(slots, axis=0)
    return highest + jnp.log2(jnp.sum(jnp.exp2(slots - highest[None]), axis=0))


def nt(a, b):
    return lax.dot_general(a, b, (((1,), (1,)), ((), ())), preferred_element_type=F32)


def nn(a, b):
    return lax.dot_general(a, b, (((1,), (0,)), ((), ())), preferred_element_type=F32)


def tn(a, b):
    return lax.dot_general(a, b, (((0,), (0,)), ((), ())), preferred_element_type=F32)


def norm_rows(points):
    norm = jnp.sum(points * points, axis=0, keepdims=True)
    first = norm.astype(BF16).astype(F32)
    second = (norm - first).astype(BF16).astype(F32)
    third = norm - first - second
    shape = (8, points.shape[1])
    row = iota(shape, 0)
    return jnp.where(row == 0, first, jnp.where(row == 1, second, jnp.where(row == 2, third, 0.0)))


def with_norms_s(points):
    ones = jnp.ones((8, points.shape[1]), F32)
    return jnp.concatenate([points, ones, norm_rows(points)], axis=0).astype(BF16)


def with_norms_t(points):
    ones = jnp.ones((8, points.shape[1]), F32)
    return jnp.concatenate([points * -2.0, norm_rows(points), ones], axis=0).astype(BF16)


def kernel(
    src_ref, tgt_ref, ls_ref, lt_ref, out_s, out_t,
    y1, y2, y3, y4, yg, p1, z1, p2, p3, p4, den, num, mapped, src_all, fa, ga, tgt_all,
    numt, mt_own, k_ref, mf, wb, ste, ssem, rsem,
):
    row, y = lax.axis_index("row"), lax.axis_index("col")
    x, z, c = row // (NZ * NC), lax.rem(row // NC, NZ), lax.rem(row, NC)
    g = x * NC + c
    zp, zi = lax.rem(z, 2), z // 2
    m = g * 2 + zp
    yc, h = lax.rem(y, 4), y // 4

    def place(px, pz, pc, py):
        return ((px * NZ + pz) * NC + pc, py)

    y_peers = [place(x, z, c, lax.rem(y + d, NY)) for d in RING8]
    y4_peers = [place(x, z, c, lax.rem(y + d, NY)) for d in (2, 1, 7)]
    z_peers = [place(x, lax.rem(z + d, NZ), c, y) for d in RING8]
    z4_peers = [place(x, lax.rem(z + d, NZ), c, y) for d in (4, 2, 6)]
    g_pos = [(lax.rem(x + dx, NX), lax.rem(c + dc, NC)) for dx, dc in PLANE]
    g_peers = [place(px, z, pc, y) for px, pc in g_pos]
    z_pair = z + 1 - 2 * zp
    far_pos = [(lax.rem(x + dx, NX), lax.rem(c + dc, NC)) for dx in (2, 1, 3, 0) for dc in (1, 0)]
    r_peers, r_index = [], []
    for dx in (2, 1, 3, 0):
        for pair in (True, False):
            for dc in (1, 0):
                if dx == 0 and dc == 0 and not pair:
                    continue
                px, pc = lax.rem(x + dx, NX), lax.rem(c + dc, NC)
                r_peers.append(place(px, z_pair if pair else z, pc, y))
                r_index.append((px * NC + pc) * 2 + ((1 - zp) if pair else zp))

    barrier = pltpu.get_barrier_semaphore()
    greeted = y_peers + z_peers + g_peers + [place(px, z_pair, pc, y) for px, pc in far_pos[:-1]]
    for peer in greeted:
        pl.semaphore_signal(barrier, inc=1, device_id=peer, device_id_type=MESH)

    def send(name, source, target, peer):
        i = IDX[name]
        pltpu.make_async_remote_copy(
            src_ref=source, dst_ref=target, send_sem=ssem.at[i], recv_sem=rsem.at[i],
            device_id=peer, device_id_type=MESH,
        ).start()

    def share(name, buf, me, peers, value):
        buf[me] = value
        for peer in peers:
            send(name, buf.at[me], buf.at[me], peer)

    def settle(sems, name, buf, n):
        span = buf.at[pl.ds(0, n)]
        pltpu.make_async_copy(span, span, sems.at[IDX[name]]).wait()

    src_t, tgt_t = src_ref[...].astype(F32), tgt_ref[...].astype(F32)
    src_own, tgt_own = with_norms_s(src_t), with_norms_t(tgt_t)
    scores = tn(tgt_own, src_own) * (-SCALE)
    highest = jnp.max(scores, axis=0, keepdims=True)
    partial = highest + jnp.log2(jnp.sum(jnp.exp2(scores - highest), axis=0, keepdims=True))

    pl.semaphore_wait(barrier, len(greeted))
    share("y1", y1, y, y_peers, partial)
    share("src", src_all, zi, z4_peers, src_t)
    tgt_all[0, y] = tgt_t[: D // 2]
    tgt_all[1, y] = tgt_t[D // 2 :]
    for peer in y_peers:
        send("tgt", tgt_all.at[c, y], tgt_all.at[c, y], peer)
    mt_own[...] = scores

    log_a = ls_ref[...] * LOG2E
    lanes_of = (iota((8, T), 1) % 8 == iota((8, T), 0)).astype(F32)
    spread = (iota((T, 128), 0) // 8 == iota((T, 128), 1)).astype(F32)
    log_b_own = lax.dot_general(
        lt_ref[...] * LOG2E * lanes_of, spread, (((1,), (0,)), ((), ())),
        preferred_element_type=F32, precision=lax.Precision.HIGHEST,
    )
    lane = iota((8, 128), 1)

    settle(rsem, "y1", y1, 7)
    f_own = log_a - lse2(y1[...])

    packed = jnp.zeros((8, 128), F32)
    for k in range(NK):
        s = mt_own[8 * k : 8 * k + 8, :] + f_own
        highest = jnp.max(s, axis=1, keepdims=True)
        total = jnp.sum(jnp.exp2(s - highest), axis=1, keepdims=True)
        packed = jnp.where(lane == k, highest + jnp.log2(total), packed)
    share("p1", p1, g, g_peers, packed)
    share("fa", fa, zi, z4_peers, jnp.concatenate([f_own, log_a], axis=1))
    settle(rsem, "p1", p1, 7)
    share("z1", z1, z, z_peers, lse2(p1[...]))

    settle(rsem, "src", src_all, 3)
    settle(rsem, "fa", fa, 3)
    mass_a = jnp.exp2(fa[:, :, S:])
    ste[D:, :] = jnp.ones((D, ZH * S), BF16)
    for zz in range(ZH):
        ste[:D, zz * S : (zz + 1) * S] = src_all[zz].astype(BF16)

    def fill(half, points):
        for zz in range(ZH):
            inner = tn(points, with_norms_s(src_all[zz]))
            k_ref[half, zz] = inner * (-SCALE) + (fa[zz][:, :S] + SHIFT)

    fill(h, tgt_own)
    settle(rsem, "tgt", tgt_all.at[0], 7)
    sibling = place(x, z, 1 - c, y)
    for d in RING8:
        other = lax.rem(y + d, NY)
        send("fwd", tgt_all.at[c, other], tgt_all.at[c, other], sibling)

    def build(half, potential, acc):
        for k in range(NK):
            block = jnp.exp2(k_ref[half, :, 8 * k : 8 * k + 8, :] + potential[:, k : k + 1])
            k_ref[half, :, 8 * k : 8 * k + 8, :] = block
            if acc is not None:
                acc = acc + block
        return acc

    def row_pass(v):
        acc = jnp.zeros((ZH, 8, S), F32)
        for half in range(YH):
            for k in range(NK):
                n = half * NK + k
                acc = acc + k_ref[half, :, 8 * k : 8 * k + 8, :] * v[:, n : n + 1]
        return jnp.sum(acc, axis=1, keepdims=True)

    def col_pass(u, keep=False):
        out = jnp.zeros((8, 128), F32)
        ub = jnp.broadcast_to(u, (ZH, 8, S))
        for half in range(YH):
            for k in range(NK):
                block = k_ref[half, :, 8 * k : 8 * k + 8, :] * ub
                if keep and k % 2 == 0:
                    before = block
                elif keep:
                    for zz in range(ZH):
                        pair = jnp.concatenate([before[zz], block[zz]], axis=0)
                        wb[half, 8 * k - 8 : 8 * k + 8, zz * S : (zz + 1) * S] = pair.astype(BF16)
                t = jnp.sum(block, axis=0)
                t = t[:, :128] + t[:, 128:]
                out = jnp.where(lane == half * NK + k, jnp.sum(t, axis=1, keepdims=True), out)
        return out

    settle(rsem, "z1", z1, 7)
    g1_own = log_b_own - lse2(z1[...])
    acc = build(h, g1_own, jnp.zeros((ZH, 8, S), F32))
    share("y2", y2, y, y_peers, jnp.sum(acc, axis=1, keepdims=True))
    ga[0] = jnp.concatenate([g1_own, log_b_own], axis=0)
    send("ga", ga.at[0], ga.at[1], place(x, z, c, lax.rem(y + 4, NY)))
    settle(rsem, "fwd", tgt_all.at[0], 7)

    def full(yy, carry):
        block = jnp.concatenate([tgt_all[0, yy], tgt_all[1, yy]], axis=0)
        mf[yy] = tn(with_norms_t(block), src_own) * (-SCALE)
        return carry

    other = lax.rem(y + 4, NY)
    fill(1 - h, with_norms_t(jnp.concatenate([tgt_all[0, other], tgt_all[1, other]], axis=0)))
    settle(rsem, "ga", ga, 1)
    g1_far, log_b_far = ga[1][:8], ga[1][8:]

    def both_halves(own, far):
        own, far = own[:, :NK], far[:, :NK]
        return jnp.where(h == 0, jnp.concatenate([own, far], axis=1), jnp.concatenate([far, own], axis=1))

    g1 = both_halves(g1_own, g1_far)
    mass_b = jnp.exp2(both_halves(log_b_own, log_b_far))
    build(1 - h, g1_far, None)

    settle(rsem, "y2", y2, 7)
    u = mass_a / jnp.sum(y2[...], axis=0)
    share("p2", p2, m, r_peers, col_pass(u))
    lax.fori_loop(0, NY, full, 0)
    settle(rsem, "p2", p2, NR - 1)
    v = mass_b / jnp.sum(p2[...], axis=0)

    share("y3", y3, yc, y4_peers, row_pass(v))
    settle(rsem, "y3", y3, 3)
    u = mass_a / jnp.sum(y3[...], axis=0)
    share("p3", p3, m, r_peers, col_pass(u))
    settle(rsem, "p3", p3, NR - 1)
    v = mass_b / jnp.sum(p3[...], axis=0)

    share("y4", y4, yc, y4_peers, row_pass(v))
    settle(rsem, "y4", y4, 3)
    sums = jnp.sum(y4[...], axis=0)
    u = mass_a / sums
    share("p4", p4, m, r_peers, col_pass(u, keep=True))
    weighted = nt(ste[...], wb[h])
    den[m] = weighted[D : D + 1]
    for n in range(NR):
        numt[n] = weighted[n * FR : n * FR + FR]
    num[m] = numt[m]
    for peer, index in zip(r_peers, r_index):
        send("den", den.at[m], den.at[m], peer)
        send("num", numt.at[index], num.at[m], peer)

    f_last = f_own + log_a - jnp.log2(jnp.sum(y4[:, zi], axis=0)) + SHIFT

    def add_f(yy, carry):
        mf[yy] = mf[yy] + f_last
        return carry

    lax.fori_loop(0, NY, add_f, 0)
    settle(rsem, "p4", p4, NR - 1)
    g4 = g1 + jnp.log2(mass_b / jnp.sum(p4[...], axis=0))
    share("yg", yg, yc, y4_peers, g4)

    settle(rsem, "den", den, NR - 1)
    settle(rsem, "num", num, NR - 1)
    share("map", mapped, m, r_peers, jnp.sum(num[...], axis=0) / jnp.sum(den[...], axis=0))

    settle(rsem, "yg", yg, 3)

    def finish(cls, acc):
        potential = yg[cls]
        for half in range(YH):
            yy = cls + 4 * half
            parts = []
            for k in range(NK):
                n = half * NK + k
                parts.append(jnp.exp2(mf[yy, 8 * k : 8 * k + 8, :] + potential[:, n : n + 1]))
            weight = jnp.concatenate(parts, axis=0).astype(BF16)
            block = jnp.concatenate([tgt_all[0, yy], tgt_all[1, yy], jnp.ones((D, T), F32)], axis=0)
            acc = acc + nn(block.astype(BF16), weight)
        return acc

    both = lax.fori_loop(0, 4, finish, jnp.zeros((2 * D, S), F32))
    out_s[...] = both[:D] / both[D:]

    settle(rsem, "map", mapped, NR - 1)
    for n in range(NR):
        out_t[n * FR : n * FR + FR, :] = mapped[n]

    for name, buf, n in (
        ("y1", y1, 7), ("y2", y2, 7), ("y3", y3, 3), ("y4", y4, 3), ("yg", yg, 3), ("p1", p1, 7), ("z1", z1, 7),
        ("p2", p2, NR - 1), ("p3", p3, NR - 1), ("p4", p4, NR - 1), ("den", den, NR - 1), ("num", num, NR - 1),
        ("map", mapped, NR - 1), ("src", src_all, 3), ("fa", fa, 3), ("ga", ga, 1),
        ("tgt", tgt_all.at[0], 7), ("fwd", tgt_all.at[0], 7),
    ):
        settle(ssem, name, buf, n)


def per_device(source, target, log_source, log_target):
    vmem = pl.BlockSpec(memory_space=pltpu.VMEM)
    n = len(PHASES)
    scratch = [
        pltpu.VMEM((NY, 1, S), F32),
        pltpu.VMEM((NY, ZH, 1, S), F32),
        pltpu.VMEM((4, ZH, 1, S), F32),
        pltpu.VMEM((4, ZH, 1, S), F32),
        pltpu.VMEM((4, 8, 128), F32),
        pltpu.VMEM((NG, 8, 128), F32),
        pltpu.VMEM((NZ, 8, 128), F32),
        pltpu.VMEM((NR, 8, 128), F32),
        pltpu.VMEM((NR, 8, 128), F32),
        pltpu.VMEM((NR, 8, 128), F32),
        pltpu.VMEM((NR, 1, T), F32),
        pltpu.VMEM((NR, FR, T), F32),
        pltpu.VMEM((NR, FR, T), F32),
        pltpu.VMEM((ZH, D, S), F32),
        pltpu.VMEM((ZH, 1, 2 * S), F32),
        pltpu.VMEM((2, 16, 128), F32),
        pltpu.VMEM((2, NY, D // 2, T), F32),
        pltpu.VMEM((NR, FR, T), F32),
        pltpu.VMEM((T, S), F32),
        pltpu.VMEM((YH, ZH, T, S), F32),
        pltpu.VMEM((NY, T, S), F32),
        pltpu.VMEM((YH, T, ZH * S), BF16),
        pltpu.VMEM((2 * D, ZH * S), BF16),
        pltpu.SemaphoreType.DMA((n,)),
        pltpu.SemaphoreType.DMA((n,)),
    ]
    source_map, target_map = pl.pallas_call(
        kernel,
        out_shape=(jax.ShapeDtypeStruct((D, S), F32), jax.ShapeDtypeStruct((D, T), F32)),
        in_specs=[vmem] * 4,
        out_specs=(vmem, vmem),
        scratch_shapes=scratch,
        compiler_params=pltpu.CompilerParams(
            collective_id=0, has_side_effects=True, vmem_limit_bytes=48 * 1024 * 1024
        ),
    )(source.T, target.T, log_source.reshape(1, S), log_target.reshape(1, T))
    return source_map.T, target_map.T


def solution(mesh):
    in_specs = (P("row", None), P("col", None), P("row"), P("col"))
    out_specs = (P("row", None), P("col", None))
    return jax.shard_map(
        per_device, mesh=mesh, in_specs=in_specs, out_specs=out_specs, check_vma=False
    )
```

```python
import jax
import jax.numpy as jnp
from jax import lax
from jax.experimental import pallas as pl
from jax.experimental.pallas import tpu as pltpu
from jax.sharding import PartitionSpec as P

EPS = 3.0
LOG2E = 1.4426950408889634
SCALE = LOG2E / EPS
SHIFT = 40.0

NX, NZ, NC, NY = 4, 8, 2, 8
NG = NX * NC
ZH, YH = 4, 2
NR = NG * 2
FR = 64 // NR
S, T, D = 256, 512, 64
NK = T // 8
F32, BF16 = jnp.float32, jnp.bfloat16
MESH = pl.DeviceIdType.MESH
RING8 = (4, 3, 5, 2, 6, 1, 7)
PLANE = tuple((dx, dc) for dx in (2, 1, 3) for dc in (1, 0)) + ((0, 1),)

PHASES = (
    "y1", "y2", "y3", "y4", "yg", "p1", "z1", "p2", "p3", "p4", "den", "num", "map", "src", "fa", "ga", "tgt", "fwd",
    "tgb", "fwb",
)
IDX = {name: i for i, name in enumerate(PHASES)}


def iota(shape, dim):
    return lax.broadcasted_iota(jnp.int32, shape, dim)


def lse2(slots):
    highest = jnp.max(slots, axis=0)
    return highest + jnp.log2(jnp.sum(jnp.exp2(slots - highest[None]), axis=0))


def nt(a, b):
    return lax.dot_general(a, b, (((1,), (1,)), ((), ())), preferred_element_type=F32)


def nn(a, b):
    return lax.dot_general(a, b, (((1,), (0,)), ((), ())), preferred_element_type=F32)


def tn(a, b):
    return lax.dot_general(a, b, (((0,), (0,)), ((), ())), preferred_element_type=F32)


def norm_rows(points):
    norm = jnp.sum(points * points, axis=0, keepdims=True)
    first = norm.astype(BF16).astype(F32)
    second = (norm - first).astype(BF16).astype(F32)
    third = norm - first - second
    shape = (8, points.shape[1])
    row = iota(shape, 0)
    return jnp.where(row == 0, first, jnp.where(row == 1, second, jnp.where(row == 2, third, 0.0)))


def with_norms_s(points):
    ones = jnp.ones((8, points.shape[1]), F32)
    return jnp.concatenate([points, ones, norm_rows(points)], axis=0).astype(BF16)


def with_norms_t(points):
    ones = jnp.ones((8, points.shape[1]), F32)
    return jnp.concatenate([points * -2.0, norm_rows(points), ones], axis=0).astype(BF16)


def kernel(
    src_hbm, tgt_hbm, ls_hbm, lt_hbm, out_s, out_t,
    y1, y2, y3, y4, yg, p1, z1, p2, p3, p4, den, num, mapped, src_all, fa, ga, tgt_all,
    numt, mt_own, k_ref, mf, wb, ste, src_ref, tgt_ref, ls_ref, lt_ref, ssem, rsem, isem,
):
    row, y = lax.axis_index("row"), lax.axis_index("col")
    x, z, c = row // (NZ * NC), lax.rem(row // NC, NZ), lax.rem(row, NC)
    g = x * NC + c
    zp, zi = lax.rem(z, 2), z // 2
    m = g * 2 + zp
    yc, h = lax.rem(y, 4), y // 4

    def place(px, pz, pc, py):
        return ((px * NZ + pz) * NC + pc, py)

    y_peers = [place(x, z, c, lax.rem(y + d, NY)) for d in RING8]
    y4_peers = [place(x, z, c, lax.rem(y + d, NY)) for d in (2, 1, 7)]
    z_peers = [place(x, lax.rem(z + d, NZ), c, y) for d in RING8]
    z4_peers = [place(x, lax.rem(z + d, NZ), c, y) for d in (4, 2, 6)]
    g_pos = [(lax.rem(x + dx, NX), lax.rem(c + dc, NC)) for dx, dc in PLANE]
    g_peers = [place(px, z, pc, y) for px, pc in g_pos]
    z_pair = z + 1 - 2 * zp
    far_pos = [(lax.rem(x + dx, NX), lax.rem(c + dc, NC)) for dx in (2, 1, 3, 0) for dc in (1, 0)]
    r_peers, r_index = [], []
    for dx in (2, 1, 3, 0):
        for pair in (True, False):
            for dc in (1, 0):
                if dx == 0 and dc == 0 and not pair:
                    continue
                px, pc = lax.rem(x + dx, NX), lax.rem(c + dc, NC)
                r_peers.append(place(px, z_pair if pair else z, pc, y))
                r_index.append((px * NC + pc) * 2 + ((1 - zp) if pair else zp))

    loads = [
        pltpu.make_async_copy(a, b, isem.at[i])
        for i, (a, b) in enumerate(
            ((src_hbm, src_ref), (tgt_hbm, tgt_ref), (ls_hbm, ls_ref), (lt_hbm, lt_ref))
        )
    ]
    for load in loads:
        load.start()
    barrier = pltpu.get_barrier_semaphore()
    greeted = y_peers + z_peers + g_peers + [place(px, z_pair, pc, y) for px, pc in far_pos[:-1]]
    for peer in greeted:
        pl.semaphore_signal(barrier, inc=1, device_id=peer, device_id_type=MESH)

    def send(name, source, target, peer):
        i = IDX[name]
        pltpu.make_async_remote_copy(
            src_ref=source, dst_ref=target, send_sem=ssem.at[i], recv_sem=rsem.at[i],
            device_id=peer, device_id_type=MESH,
        ).start()

    def share(name, buf, me, peers, value):
        buf[me] = value
        for peer in peers:
            send(name, buf.at[me], buf.at[me], peer)

    def settle(sems, name, buf, n):
        span = buf.at[pl.ds(0, n)]
        pltpu.make_async_copy(span, span, sems.at[IDX[name]]).wait()

    for load in loads:
        load.wait()
    src_t, tgt_t = src_ref[...].astype(F32), tgt_ref[...].astype(F32)
    src_own, tgt_own = with_norms_s(src_t), with_norms_t(tgt_t)
    scores = tn(tgt_own, src_own) * (-SCALE)
    highest = jnp.max(scores, axis=0, keepdims=True)
    partial = highest + jnp.log2(jnp.sum(jnp.exp2(scores - highest), axis=0, keepdims=True))

    pl.semaphore_wait(barrier, len(greeted))
    share("y1", y1, y, y_peers, partial)
    share("src", src_all, zi, z4_peers, src_t)
    tgt_all[0, y] = tgt_t[: D // 2]
    tgt_all[1, y] = tgt_t[D // 2 :]
    mt_own[...] = scores

    log_a = ls_ref[...] * LOG2E
    lanes_of = (iota((8, T), 1) % 8 == iota((8, T), 0)).astype(F32)
    spread = (iota((T, 128), 0) // 8 == iota((T, 128), 1)).astype(F32)
    log_b_own = lax.dot_general(
        lt_ref[...] * LOG2E * lanes_of, spread, (((1,), (0,)), ((), ())),
        preferred_element_type=F32, precision=lax.Precision.HIGHEST,
    )
    lane = iota((8, 128), 1)

    settle(rsem, "y1", y1, 7)
    for peer in y_peers[:3]:
        send("tgt", tgt_all.at[c, y], tgt_all.at[c, y], peer)
    f_own = log_a - lse2(y1[...])

    packed = jnp.zeros((8, 128), F32)
    for k in range(NK):
        s = mt_own[8 * k : 8 * k + 8, :] + f_own
        highest = jnp.max(s, axis=1, keepdims=True)
        total = jnp.sum(jnp.exp2(s - highest), axis=1, keepdims=True)
        packed = jnp.where(lane == k, highest + jnp.log2(total), packed)
    share("p1", p1, g, g_peers, packed)
    share("fa", fa, zi, z4_peers, jnp.concatenate([f_own, log_a], axis=1))
    settle(rsem, "p1", p1, 7)
    share("z1", z1, z, z_peers, lse2(p1[...]))

    settle(rsem, "src", src_all, 3)
    settle(rsem, "fa", fa, 3)
    mass_a = jnp.exp2(fa[:, :, S:])
    ste[D:, :] = jnp.ones((D, ZH * S), BF16)
    for zz in range(ZH):
        ste[:D, zz * S : (zz + 1) * S] = src_all[zz].astype(BF16)

    def fill(half, points):
        for zz in range(ZH):
            inner = tn(points, with_norms_s(src_all[zz]))
            k_ref[half, zz] = inner * (-SCALE) + (fa[zz][:, :S] + SHIFT)

    fill(h, tgt_own)
    sibling = place(x, z, 1 - c, y)

    def forward(arrived, name, distances):
        settle(rsem, arrived, tgt_all.at[0], len(distances))
        for d in distances:
            other = lax.rem(y + d, NY)
            send(name, tgt_all.at[c, other], tgt_all.at[c, other], sibling)

    forward("tgt", "fwd", RING8[:3])

    def build(half, potential, acc):
        for k in range(NK):
            block = jnp.exp2(k_ref[half, :, 8 * k : 8 * k + 8, :] + potential[:, k : k + 1])
            k_ref[half, :, 8 * k : 8 * k + 8, :] = block
            if acc is not None:
                acc = acc + block
        return acc

    def row_pass(v):
        acc = jnp.zeros((ZH, 8, S), F32)
        for half in range(YH):
            for k in range(NK):
                n = half * NK + k
                acc = acc + k_ref[half, :, 8 * k : 8 * k + 8, :] * v[:, n : n + 1]
        return jnp.sum(acc, axis=1, keepdims=True)

    def col_half(half, u, first, out, keep=False):
        ub = jnp.broadcast_to(u, (ZH, 8, S))
        for k in range(NK):
            block = k_ref[half, :, 8 * k : 8 * k + 8, :] * ub
            if keep and k % 2 == 0:
                before = block
            elif keep:
                for zz in range(ZH):
                    pair = jnp.concatenate([before[zz], block[zz]], axis=0)
                    wb[8 * k - 8 : 8 * k + 8, zz * S : (zz + 1) * S] = pair.astype(BF16)
            t = jnp.sum(block, axis=0)
            t = t[:, :128] + t[:, 128:]
            out = jnp.where(lane == first + k, jnp.sum(t, axis=1, keepdims=True), out)
        return out

    def col_pass(u):
        return col_half(1, u, NK, col_half(0, u, 0, jnp.zeros((8, 128), F32)))

    settle(rsem, "z1", z1, 7)
    g1_own = log_b_own - lse2(z1[...])
    acc = build(h, g1_own, jnp.zeros((ZH, 8, S), F32))
    share("y2", y2, y, y_peers, jnp.sum(acc, axis=1, keepdims=True))
    ga[0] = jnp.concatenate([g1_own, log_b_own], axis=0)
    send("ga", ga.at[0], ga.at[1], place(x, z, c, lax.rem(y + 4, NY)))
    settle(rsem, "fwd", tgt_all.at[0], 3)

    def full(yy, carry):
        block = jnp.concatenate([tgt_all[0, yy], tgt_all[1, yy]], axis=0)
        mf[yy] = tn(with_norms_t(block), src_own) * (-SCALE)
        return carry

    other = lax.rem(y + 4, NY)
    fill(1 - h, with_norms_t(jnp.concatenate([tgt_all[0, other], tgt_all[1, other]], axis=0)))
    settle(rsem, "ga", ga, 1)
    g1_far, log_b_far = ga[1][:8], ga[1][8:]

    def both_halves(own, far):
        own, far = own[:, :NK], far[:, :NK]
        return jnp.where(h == 0, jnp.concatenate([own, far], axis=1), jnp.concatenate([far, own], axis=1))

    g1 = both_halves(g1_own, g1_far)
    mass_b = jnp.exp2(both_halves(log_b_own, log_b_far))
    build(1 - h, g1_far, None)

    settle(rsem, "y2", y2, 7)
    for peer in y_peers[3:]:
        send("tgb", tgt_all.at[c, y], tgt_all.at[c, y], peer)
    u = mass_a / jnp.sum(y2[...], axis=0)
    share("p2", p2, m, r_peers, col_pass(u))
    settle(rsem, "p2", p2, NR - 1)
    v = mass_b / jnp.sum(p2[...], axis=0)

    share("y3", y3, yc, y4_peers, row_pass(v))
    settle(rsem, "y3", y3, 3)
    u = mass_a / jnp.sum(y3[...], axis=0)
    share("p3", p3, m, r_peers, col_pass(u))
    forward("tgb", "fwb", RING8[3:])
    settle(rsem, "p3", p3, NR - 1)
    v = mass_b / jnp.sum(p3[...], axis=0)

    share("y4", y4, yc, y4_peers, row_pass(v))
    settle(rsem, "fwb", tgt_all.at[0], 4)
    lax.fori_loop(0, NY, full, 0)
    settle(rsem, "y4", y4, 3)
    sums = jnp.sum(y4[...], axis=0)
    u = mass_a / sums
    nothing = jnp.zeros((8, 128), F32)
    sums_own = col_half(h, u, 0, nothing, keep=True)
    weighted = nt(ste[...], wb[...])
    for n in range(NR):
        numt[n] = weighted[n * FR : n * FR + FR]
    num[m] = numt[m]
    for peer, index in zip(r_peers, r_index):
        send("num", numt.at[index], num.at[m], peer)
    share("p4", p4, m, r_peers, both_halves(sums_own, col_half(1 - h, u, 0, nothing)))
    share("den", den, m, r_peers, weighted[D : D + 1])

    f_last = f_own + log_a - jnp.log2(jnp.sum(y4[:, zi], axis=0)) + SHIFT

    def add_f(yy, carry):
        mf[yy] = mf[yy] + f_last
        return carry

    lax.fori_loop(0, NY, add_f, 0)
    settle(rsem, "p4", p4, NR - 1)
    g4 = g1 + jnp.log2(mass_b / jnp.sum(p4[...], axis=0))
    share("yg", yg, yc, y4_peers, g4)

    settle(rsem, "num", num, NR - 1)
    share("map", mapped, m, r_peers, jnp.sum(num[...], axis=0))

    settle(rsem, "yg", yg, 3)

    def finish(cls, acc):
        potential = yg[cls]
        for half in range(YH):
            yy = cls + 4 * half
            parts = []
            for k in range(NK):
                n = half * NK + k
                parts.append(jnp.exp2(mf[yy, 8 * k : 8 * k + 8, :] + potential[:, n : n + 1]))
            weight = jnp.concatenate(parts, axis=0).astype(BF16)
            block = jnp.concatenate([tgt_all[0, yy], tgt_all[1, yy], jnp.ones((D, T), F32)], axis=0)
            acc = acc + nn(block.astype(BF16), weight)
        return acc

    both = lax.fori_loop(0, 4, finish, jnp.zeros((2 * D, S), F32))
    out_s[...] = both[:D] / both[D:]

    settle(rsem, "den", den, NR - 1)
    total = jnp.sum(den[...], axis=0)
    settle(rsem, "map", mapped, NR - 1)
    for n in range(NR):
        out_t[n * FR : n * FR + FR, :] = mapped[n] / total

    for name, buf, n in (
        ("y1", y1, 7), ("y2", y2, 7), ("y3", y3, 3), ("y4", y4, 3), ("yg", yg, 3), ("p1", p1, 7), ("z1", z1, 7),
        ("p2", p2, NR - 1), ("p3", p3, NR - 1), ("p4", p4, NR - 1), ("den", den, NR - 1), ("num", num, NR - 1),
        ("map", mapped, NR - 1), ("src", src_all, 3), ("fa", fa, 3), ("ga", ga, 1),
        ("tgt", tgt_all.at[0], 3), ("fwd", tgt_all.at[0], 3), ("tgb", tgt_all.at[0], 4), ("fwb", tgt_all.at[0], 4),
    ):
        settle(ssem, name, buf, n)


def deliver(s_in, t_in, s_out, t_out, sems):
    copies = [
        pltpu.make_async_copy(s_in, s_out, sems.at[0]),
        pltpu.make_async_copy(t_in, t_out, sems.at[1]),
    ]
    for copy in copies:
        copy.start()
    for copy in copies:
        copy.wait()


def per_device(source, target, log_source, log_target):
    vmem = pl.BlockSpec(memory_space=pltpu.VMEM)
    n = len(PHASES)
    scratch = [
        pltpu.VMEM((NY, 1, S), F32),
        pltpu.VMEM((NY, ZH, 1, S), F32),
        pltpu.VMEM((4, ZH, 1, S), F32),
        pltpu.VMEM((4, ZH, 1, S), F32),
        pltpu.VMEM((4, 8, 128), F32),
        pltpu.VMEM((NG, 8, 128), F32),
        pltpu.VMEM((NZ, 8, 128), F32),
        pltpu.VMEM((NR, 8, 128), F32),
        pltpu.VMEM((NR, 8, 128), F32),
        pltpu.VMEM((NR, 8, 128), F32),
        pltpu.VMEM((NR, 1, T), F32),
        pltpu.VMEM((NR, FR, T), F32),
        pltpu.VMEM((NR, FR, T), F32),
        pltpu.VMEM((ZH, D, S), F32),
        pltpu.VMEM((ZH, 1, 2 * S), F32),
        pltpu.VMEM((2, 16, 128), F32),
        pltpu.VMEM((2, NY, D // 2, T), F32),
        pltpu.VMEM((NR, FR, T), F32),
        pltpu.VMEM((T, S), F32),
        pltpu.VMEM((YH, ZH, T, S), F32),
        pltpu.VMEM((NY, T, S), F32),
        pltpu.VMEM((T, ZH * S), BF16),
        pltpu.VMEM((2 * D, ZH * S), BF16),
        pltpu.VMEM((D, S), BF16),
        pltpu.VMEM((D, T), BF16),
        pltpu.VMEM((1, S), F32),
        pltpu.VMEM((1, T), F32),
        pltpu.SemaphoreType.DMA((n,)),
        pltpu.SemaphoreType.DMA((n,)),
        pltpu.SemaphoreType.DMA((4,)),
    ]
    source_map, target_map = pl.pallas_call(
        kernel,
        out_shape=(pltpu.VMEM((D, S), F32), pltpu.VMEM((D, T), F32)),
        in_specs=[pl.BlockSpec(memory_space=pltpu.HBM)] * 4,
        out_specs=(vmem, vmem),
        scratch_shapes=scratch,
        compiler_params=pltpu.CompilerParams(
            collective_id=0, has_side_effects=True, vmem_limit_bytes=62 * 1024 * 1024
        ),
    )(source.T, target.T, log_source.reshape(1, S), log_target.reshape(1, T))
    source_map, target_map = pl.pallas_call(
        deliver,
        out_shape=(jax.ShapeDtypeStruct((D, S), F32), jax.ShapeDtypeStruct((D, T), F32)),
        in_specs=[pl.BlockSpec(memory_space=pltpu.VMEM)] * 2,
        out_specs=(pl.BlockSpec(memory_space=pl.ANY),) * 2,
        scratch_shapes=[pltpu.SemaphoreType.DMA((2,))],
        compiler_params=pltpu.CompilerParams(vmem_limit_bytes=2 * 1024 * 1024),
    )(source_map, target_map)
    return source_map.T, target_map.T


def solution(mesh):
    in_specs = (P("row", None), P("col", None), P("row"), P("col"))
    out_specs = (P("row", None), P("col", None))
    return jax.shard_map(
        per_device, mesh=mesh, in_specs=in_specs, out_specs=out_specs, check_vma=False
    )
```

```python
import jax
import jax.numpy as jnp
from jax import lax
from jax.experimental import pallas as pl
from jax.experimental.pallas import tpu as pltpu
from jax.sharding import PartitionSpec as P

EPS = 3.0
LOG2E = 1.4426950408889634
SCALE = LOG2E / EPS
SHIFT = 40.0

NX, NZ, NC, NY = 4, 8, 2, 8
NG = NX * NC
ZH, YH = 4, 2
NR = NG * 2
FR = 64 // NR
S, T, D = 256, 512, 64
NK = T // 8
F32, BF16 = jnp.float32, jnp.bfloat16
MESH = pl.DeviceIdType.MESH
RING8 = (4, 3, 5, 2, 6, 1, 7)
PLANE = tuple((dx, dc) for dx in (2, 1, 3) for dc in (1, 0)) + ((0, 1),)

PHASES = (
    "y1", "y2", "y3", "y4", "p1", "z1", "p2", "p3", "p4", "den", "num", "map", "src", "fa", "ga", "tgt", "fwd",
    "tgb", "fwb",
)
IDX = {name: i for i, name in enumerate(PHASES)}


def iota(shape, dim):
    return lax.broadcasted_iota(jnp.int32, shape, dim)


def lse2(slots):
    highest = jnp.max(slots, axis=0)
    return highest + jnp.log2(jnp.sum(jnp.exp2(slots - highest[None]), axis=0))


def nt(a, b):
    return lax.dot_general(a, b, (((1,), (1,)), ((), ())), preferred_element_type=F32)


def nn(a, b):
    return lax.dot_general(a, b, (((1,), (0,)), ((), ())), preferred_element_type=F32)


def tn(a, b):
    return lax.dot_general(a, b, (((0,), (0,)), ((), ())), preferred_element_type=F32)


def norm_rows(points):
    norm = jnp.sum(points * points, axis=0, keepdims=True)
    first = norm.astype(BF16).astype(F32)
    second = (norm - first).astype(BF16).astype(F32)
    third = norm - first - second
    shape = (8, points.shape[1])
    row = iota(shape, 0)
    return jnp.where(row == 0, first, jnp.where(row == 1, second, jnp.where(row == 2, third, 0.0)))


def with_norms_s(points):
    ones = jnp.ones((8, points.shape[1]), F32)
    return jnp.concatenate([points, ones, norm_rows(points)], axis=0).astype(BF16)


def with_norms_t(points):
    ones = jnp.ones((8, points.shape[1]), F32)
    return jnp.concatenate([points * -2.0, norm_rows(points), ones], axis=0).astype(BF16)


def kernel(
    src_hbm, tgt_hbm, ls_hbm, lt_hbm, out_s, out_t,
    y1, y2, y3, y4, yg, p1, z1, p2, p3, p4, den, num, mapped, src_all, fa, ga, tgt_all,
    numt, mt_own, k_ref, mf, wb, ste, src_ref, tgt_ref, ls_ref, lt_ref, both, ssem, rsem, isem, gsem,
):
    row, y = lax.axis_index("row"), lax.axis_index("col")
    x, z, c = row // (NZ * NC), lax.rem(row // NC, NZ), lax.rem(row, NC)
    g = x * NC + c
    zp, zi = lax.rem(z, 2), z // 2
    m = g * 2 + zp
    yc, h = lax.rem(y, 4), y // 4

    def place(px, pz, pc, py):
        return ((px * NZ + pz) * NC + pc, py)

    y_peers = [place(x, z, c, lax.rem(y + d, NY)) for d in RING8]
    y4_peers = [place(x, z, c, lax.rem(y + d, NY)) for d in (2, 1, 7)]
    z_peers = [place(x, lax.rem(z + d, NZ), c, y) for d in RING8]
    z4_peers = [place(x, lax.rem(z + d, NZ), c, y) for d in (4, 2, 6)]
    g_pos = [(lax.rem(x + dx, NX), lax.rem(c + dc, NC)) for dx, dc in PLANE]
    g_peers = [place(px, z, pc, y) for px, pc in g_pos]
    z_pair = z + 1 - 2 * zp
    far_pos = [(lax.rem(x + dx, NX), lax.rem(c + dc, NC)) for dx in (2, 1, 3, 0) for dc in (1, 0)]
    r_peers, r_index = [], []
    for dx in (2, 1, 3, 0):
        for pair in (True, False):
            for dc in (1, 0):
                if dx == 0 and dc == 0 and not pair:
                    continue
                px, pc = lax.rem(x + dx, NX), lax.rem(c + dc, NC)
                r_peers.append(place(px, z_pair if pair else z, pc, y))
                r_index.append((px * NC + pc) * 2 + ((1 - zp) if pair else zp))

    loads = [
        pltpu.make_async_copy(a, b, isem.at[i])
        for i, (a, b) in enumerate(
            ((src_hbm, src_ref), (tgt_hbm, tgt_ref), (ls_hbm, ls_ref), (lt_hbm, lt_ref))
        )
    ]
    for load in loads:
        load.start()
    barrier = pltpu.get_barrier_semaphore()
    greeted = y_peers + z_peers + g_peers + [place(px, z_pair, pc, y) for px, pc in far_pos[:-1]]
    for peer in greeted:
        pl.semaphore_signal(barrier, inc=1, device_id=peer, device_id_type=MESH)

    def send(name, source, target, peer):
        i = IDX[name]
        pltpu.make_async_remote_copy(
            src_ref=source, dst_ref=target, send_sem=ssem.at[i], recv_sem=rsem.at[i],
            device_id=peer, device_id_type=MESH,
        ).start()

    def share(name, buf, me, peers, value):
        buf[me] = value
        for peer in peers:
            send(name, buf.at[me], buf.at[me], peer)

    def settle(sems, name, buf, n):
        span = buf.at[pl.ds(0, n)]
        pltpu.make_async_copy(span, span, sems.at[IDX[name]]).wait()

    for load in loads:
        load.wait()
    src_t, tgt_t = src_ref[...].astype(F32), tgt_ref[...].astype(F32)
    src_own, tgt_own = with_norms_s(src_t), with_norms_t(tgt_t)
    scores = tn(tgt_own, src_own) * (-SCALE)
    highest = jnp.max(scores, axis=0, keepdims=True)
    partial = highest + jnp.log2(jnp.sum(jnp.exp2(scores - highest), axis=0, keepdims=True))

    pl.semaphore_wait(barrier, len(greeted))
    share("y1", y1, y, y_peers, partial)
    share("src", src_all, zi, z4_peers, src_t)
    tgt_all[0, y] = tgt_t[: D // 2]
    tgt_all[1, y] = tgt_t[D // 2 :]
    mt_own[...] = scores

    log_a = ls_ref[...] * LOG2E
    lanes_of = (iota((8, T), 1) % 8 == iota((8, T), 0)).astype(F32)
    spread = (iota((T, 128), 0) // 8 == iota((T, 128), 1)).astype(F32)
    log_b_own = lax.dot_general(
        lt_ref[...] * LOG2E * lanes_of, spread, (((1,), (0,)), ((), ())),
        preferred_element_type=F32, precision=lax.Precision.HIGHEST,
    )
    lane = iota((8, 128), 1)

    settle(rsem, "y1", y1, 7)
    for peer in y_peers[:3]:
        send("tgt", tgt_all.at[c, y], tgt_all.at[c, y], peer)
    f_own = log_a - lse2(y1[...])

    packed = jnp.zeros((8, 128), F32)
    for k in range(NK):
        s = mt_own[8 * k : 8 * k + 8, :] + f_own
        highest = jnp.max(s, axis=1, keepdims=True)
        total = jnp.sum(jnp.exp2(s - highest), axis=1, keepdims=True)
        packed = jnp.where(lane == k, highest + jnp.log2(total), packed)
    share("p1", p1, g, g_peers, packed)
    share("fa", fa, zi, z4_peers, jnp.concatenate([f_own, log_a], axis=1))
    settle(rsem, "p1", p1, 7)
    share("z1", z1, z, z_peers, lse2(p1[...]))

    settle(rsem, "src", src_all, 3)
    settle(rsem, "fa", fa, 3)
    mass_a = jnp.exp2(fa[:, :, S:])

    def fill(half, points):
        for zz in range(ZH):
            inner = tn(points, with_norms_s(src_all[zz]))
            k_ref[half, zz] = inner * (-SCALE) + (fa[zz][:, :S] + SHIFT)

    fill(h, tgt_own)
    sibling = place(x, z, 1 - c, y)

    def forward(arrived, name, distances):
        settle(rsem, arrived, tgt_all.at[0], len(distances))
        for d in distances:
            other = lax.rem(y + d, NY)
            send(name, tgt_all.at[c, other], tgt_all.at[c, other], sibling)

    def build(half, potential, acc):
        for k in range(NK):
            block = jnp.exp2(k_ref[half, :, 8 * k : 8 * k + 8, :] + potential[:, k : k + 1])
            k_ref[half, :, 8 * k : 8 * k + 8, :] = block
            if acc is not None:
                acc = acc + block
        return acc

    def row_pass(v):
        acc = jnp.zeros((ZH, 8, S), F32)
        for half in range(YH):
            for k in range(NK):
                n = half * NK + k
                acc = acc + k_ref[half, :, 8 * k : 8 * k + 8, :] * v[:, n : n + 1]
        return jnp.sum(acc, axis=1, keepdims=True)

    def col_half(half, u, first, out):
        ub = jnp.broadcast_to(u, (ZH, 8, S))
        for k in range(NK):
            block = k_ref[half, :, 8 * k : 8 * k + 8, :] * ub
            t = jnp.sum(block, axis=0)
            t = t[:, :128] + t[:, 128:]
            out = jnp.where(lane == first + k, jnp.sum(t, axis=1, keepdims=True), out)
        return out

    def col_pass(u):
        return col_half(1, u, NK, col_half(0, u, 0, jnp.zeros((8, 128), F32)))

    settle(rsem, "z1", z1, 7)
    g1_own = log_b_own - lse2(z1[...])
    ga[0] = jnp.concatenate([g1_own, log_b_own], axis=0)
    send("ga", ga.at[0], ga.at[1], place(x, z, c, lax.rem(y + 4, NY)))
    acc = build(h, g1_own, jnp.zeros((ZH, 8, S), F32))
    share("y2", y2, y, y_peers, jnp.sum(acc, axis=1, keepdims=True))
    forward("tgt", "fwd", RING8[:3])
    settle(rsem, "fwd", tgt_all.at[0], 3)

    def full(yy, carry):
        block = jnp.concatenate([tgt_all[0, yy], tgt_all[1, yy]], axis=0)
        mf[yy] = tn(with_norms_t(block), src_own) * (-SCALE)
        return carry

    other = lax.rem(y + 4, NY)
    fill(1 - h, with_norms_t(jnp.concatenate([tgt_all[0, other], tgt_all[1, other]], axis=0)))
    settle(rsem, "ga", ga, 1)
    g1_far, log_b_far = ga[1][:8], ga[1][8:]

    def both_halves(own, far):
        own, far = own[:, :NK], far[:, :NK]
        return jnp.where(h == 0, jnp.concatenate([own, far], axis=1), jnp.concatenate([far, own], axis=1))

    g1 = both_halves(g1_own, g1_far)
    mass_b = jnp.exp2(both_halves(log_b_own, log_b_far))
    build(1 - h, g1_far, None)

    settle(rsem, "y2", y2, 7)
    for peer in y_peers[3:]:
        send("tgb", tgt_all.at[c, y], tgt_all.at[c, y], peer)
    u = mass_a / jnp.sum(y2[...], axis=0)
    share("p2", p2, m, r_peers, col_pass(u))
    settle(rsem, "p2", p2, NR - 1)
    v = mass_b / jnp.sum(p2[...], axis=0)

    share("y3", y3, yc, y4_peers, row_pass(v))
    settle(rsem, "y3", y3, 3)
    u = mass_a / jnp.sum(y3[...], axis=0)
    share("p3", p3, m, r_peers, col_pass(u))
    forward("tgb", "fwb", RING8[3:])
    settle(rsem, "p3", p3, NR - 1)
    v = mass_b / jnp.sum(p3[...], axis=0)

    share("y4", y4, yc, y4_peers, row_pass(v))
    settle(rsem, "fwb", tgt_all.at[0], 4)
    lax.fori_loop(0, NY, full, 0)
    for zz in range(ZH):
        wb[:, zz * S : (zz + 1) * S] = k_ref[h, zz].astype(BF16)
    settle(rsem, "y4", y4, 3)
    sums = jnp.sum(y4[...], axis=0)
    u = mass_a / sums
    for zz in range(ZH):
        mass = jnp.broadcast_to(u[zz], (16, S))
        scaled = jnp.concatenate([src_all[zz] * u[zz], mass], axis=0)
        high = scaled.astype(BF16)
        low = (scaled - high.astype(F32)).astype(BF16)
        ste[:, zz * S : (zz + 1) * S] = jnp.concatenate([high, low], axis=0)
    weighted = nt(ste[...], wb[...])
    weighted = weighted[: D + 16] + weighted[D + 16 :]
    for n in range(NR):
        numt[n] = weighted[n * FR : n * FR + FR]
    num[m] = numt[m]
    for peer, index in zip(r_peers, r_index):
        send("num", numt.at[index], num.at[m], peer)
    share("p4", p4, m, r_peers, col_pass(u))
    share("den", den, m, r_peers, weighted[D : D + 1])

    f_last = f_own + log_a - jnp.log2(jnp.sum(y4[:, zi], axis=0)) + SHIFT

    def add_f(yy, carry):
        mf[yy] = mf[yy] + f_last
        return carry

    lax.fori_loop(0, NY, add_f, 0)
    settle(rsem, "p4", p4, NR - 1)
    g4 = g1 + jnp.log2(mass_b / jnp.sum(p4[...], axis=0))
    yg[yc] = g4
    for i, peer in enumerate(y4_peers):
        pltpu.make_async_remote_copy(
            src_ref=yg.at[yc], dst_ref=yg.at[yc], send_sem=gsem.at[i], recv_sem=gsem.at[3 + i],
            device_id=peer, device_id_type=MESH,
        ).start()

    settle(rsem, "num", num, NR - 1)
    share("map", mapped, m, r_peers, jnp.sum(num[...], axis=0))

    def finish(cls):
        potential = yg[cls]
        acc = jnp.zeros((2 * D, S), F32)
        for half in range(YH):
            yy = cls + 4 * half
            parts = []
            for k in range(NK):
                n = half * NK + k
                parts.append(jnp.exp2(mf[yy, 8 * k : 8 * k + 8, :] + potential[:, n : n + 1]))
            weight = jnp.concatenate(parts, axis=0).astype(BF16)
            block = jnp.concatenate([tgt_all[0, yy], tgt_all[1, yy], jnp.ones((D, T), F32)], axis=0)
            acc = acc + nn(block.astype(BF16), weight)
        both[cls] = acc

    finish(yc)
    for i, d in ((2, 1), (1, 7), (0, 6)):
        cls = lax.rem(y + d, 4)
        pltpu.make_async_copy(yg.at[cls], yg.at[cls], gsem.at[3 + i]).wait()
        finish(cls)
    maps = jnp.sum(both[...], axis=0)
    out_s[...] = maps[:D] / maps[D:]

    settle(rsem, "den", den, NR - 1)
    total = jnp.sum(den[...], axis=0)
    settle(rsem, "map", mapped, NR - 1)
    for n in range(NR):
        out_t[n * FR : n * FR + FR, :] = mapped[n] / total

    for name, buf, n in (
        ("y1", y1, 7), ("y2", y2, 7), ("y3", y3, 3), ("y4", y4, 3), ("p1", p1, 7), ("z1", z1, 7),
        ("p2", p2, NR - 1), ("p3", p3, NR - 1), ("p4", p4, NR - 1), ("den", den, NR - 1), ("num", num, NR - 1),
        ("map", mapped, NR - 1), ("src", src_all, 3), ("fa", fa, 3), ("ga", ga, 1),
        ("tgt", tgt_all.at[0], 3), ("fwd", tgt_all.at[0], 3), ("tgb", tgt_all.at[0], 4), ("fwb", tgt_all.at[0], 4),
    ):
        settle(ssem, name, buf, n)
    for i in range(3):
        pltpu.make_async_copy(yg.at[0], yg.at[0], gsem.at[i]).wait()


def deliver(s_in, t_in, s_out, t_out, sems):
    copies = [
        pltpu.make_async_copy(s_in, s_out, sems.at[0]),
        pltpu.make_async_copy(t_in, t_out, sems.at[1]),
    ]
    for copy in copies:
        copy.start()
    for copy in copies:
        copy.wait()


def per_device(source, target, log_source, log_target):
    vmem = pl.BlockSpec(memory_space=pltpu.VMEM)
    n = len(PHASES)
    scratch = [
        pltpu.VMEM((NY, 1, S), F32),
        pltpu.VMEM((NY, ZH, 1, S), F32),
        pltpu.VMEM((4, ZH, 1, S), F32),
        pltpu.VMEM((4, ZH, 1, S), F32),
        pltpu.VMEM((4, 8, 128), F32),
        pltpu.VMEM((NG, 8, 128), F32),
        pltpu.VMEM((NZ, 8, 128), F32),
        pltpu.VMEM((NR, 8, 128), F32),
        pltpu.VMEM((NR, 8, 128), F32),
        pltpu.VMEM((NR, 8, 128), F32),
        pltpu.VMEM((NR, 1, T), F32),
        pltpu.VMEM((NR, FR, T), F32),
        pltpu.VMEM((NR, FR, T), F32),
        pltpu.VMEM((ZH, D, S), F32),
        pltpu.VMEM((ZH, 1, 2 * S), F32),
        pltpu.VMEM((2, 16, 128), F32),
        pltpu.VMEM((2, NY, D // 2, T), F32),
        pltpu.VMEM((NR, FR, T), F32),
        pltpu.VMEM((T, S), F32),
        pltpu.VMEM((YH, ZH, T, S), F32),
        pltpu.VMEM((NY, T, S), F32),
        pltpu.VMEM((T, ZH * S), BF16),
        pltpu.VMEM((2 * (D + 16), ZH * S), BF16),
        pltpu.VMEM((D, S), BF16),
        pltpu.VMEM((D, T), BF16),
        pltpu.VMEM((1, S), F32),
        pltpu.VMEM((1, T), F32),
        pltpu.VMEM((4, 2 * D, S), F32),
        pltpu.SemaphoreType.DMA((n,)),
        pltpu.SemaphoreType.DMA((n,)),
        pltpu.SemaphoreType.DMA((4,)),
        pltpu.SemaphoreType.DMA((6,)),
    ]
    source_map, target_map = pl.pallas_call(
        kernel,
        out_shape=(pltpu.VMEM((D, S), F32), pltpu.VMEM((D, T), F32)),
        in_specs=[pl.BlockSpec(memory_space=pltpu.HBM)] * 4,
        out_specs=(vmem, vmem),
        scratch_shapes=scratch,
        compiler_params=pltpu.CompilerParams(
            collective_id=0, has_side_effects=True, vmem_limit_bytes=62 * 1024 * 1024
        ),
    )(source.T, target.T, log_source.reshape(1, S), log_target.reshape(1, T))
    source_map, target_map = pl.pallas_call(
        deliver,
        out_shape=(jax.ShapeDtypeStruct((D, S), F32), jax.ShapeDtypeStruct((D, T), F32)),
        in_specs=[pl.BlockSpec(memory_space=pltpu.VMEM)] * 2,
        out_specs=(pl.BlockSpec(memory_space=pl.ANY),) * 2,
        scratch_shapes=[pltpu.SemaphoreType.DMA((2,))],
        compiler_params=pltpu.CompilerParams(vmem_limit_bytes=2 * 1024 * 1024),
    )(source_map, target_map)
    return source_map.T, target_map.T


def solution(mesh):
    in_specs = (P("row", None), P("col", None), P("row"), P("col"))
    out_specs = (P("row", None), P("col", None))
    return jax.shard_map(
        per_device, mesh=mesh, in_specs=in_specs, out_specs=out_specs, check_vma=False
    )
```

```python
import jax
import jax.numpy as jnp
from jax import lax
from jax.experimental import pallas as pl
from jax.experimental.pallas import tpu as pltpu
from jax.sharding import PartitionSpec as P

EPS = 3.0
LOG2E = 1.4426950408889634
SCALE = LOG2E / EPS
SHIFT = 40.0

NX, NZ, NC, NY = 4, 8, 2, 8
NG = NX * NC
ZH, YH = 4, 2
NR = NG * 2
FR = 64 // NR
S, T, D = 256, 512, 64
NK = T // 8
F32, BF16 = jnp.float32, jnp.bfloat16
MESH = pl.DeviceIdType.MESH
RING8 = (4, 3, 5, 2, 6, 1, 7)
PLANE = tuple((dx, dc) for dx in (2, 1, 3) for dc in (1, 0)) + ((0, 1),)

PHASES = (
    "y1", "y2", "y3", "y4", "p1", "z1", "p2", "p3", "p4", "den", "num", "map", "src", "fa", "ga", "tgt", "fwd",
    "tgb", "fwb",
)
IDX = {name: i for i, name in enumerate(PHASES)}


def iota(shape, dim):
    return lax.broadcasted_iota(jnp.int32, shape, dim)


def lse2(slots):
    highest = jnp.max(slots, axis=0)
    return highest + jnp.log2(jnp.sum(jnp.exp2(slots - highest[None]), axis=0))


def nt(a, b):
    return lax.dot_general(a, b, (((1,), (1,)), ((), ())), preferred_element_type=F32)


def nn(a, b):
    return lax.dot_general(a, b, (((1,), (0,)), ((), ())), preferred_element_type=F32)


def tn(a, b):
    return lax.dot_general(a, b, (((0,), (0,)), ((), ())), preferred_element_type=F32)


def norm_rows(points):
    norm = jnp.sum(points * points, axis=0, keepdims=True)
    first = norm.astype(BF16).astype(F32)
    second = (norm - first).astype(BF16).astype(F32)
    third = norm - first - second
    shape = (8, points.shape[1])
    row = iota(shape, 0)
    return jnp.where(row == 0, first, jnp.where(row == 1, second, jnp.where(row == 2, third, 0.0)))


def with_norms_s(points):
    ones = jnp.ones((8, points.shape[1]), F32)
    return jnp.concatenate([points, ones, norm_rows(points)], axis=0).astype(BF16)


def with_norms_t(points):
    ones = jnp.ones((8, points.shape[1]), F32)
    return jnp.concatenate([points * -2.0, norm_rows(points), ones], axis=0).astype(BF16)


def kernel(
    src_hbm, tgt_hbm, ls_hbm, lt_hbm, out_s, out_t,
    y1, y2, y3, y4, yg, p1, z1, p2, p3, p4, den, num, mapped, src_all, fa, ga, tgt_all,
    numt, mt_own, k_ref, mf, wb, ste, src_ref, tgt_ref, ls_ref, lt_ref, both, ssem, rsem, isem, gsem,
):
    row, y = lax.axis_index("row"), lax.axis_index("col")
    x, z, c = row // (NZ * NC), lax.rem(row // NC, NZ), lax.rem(row, NC)
    g = x * NC + c
    zp, zi = lax.rem(z, 2), z // 2
    m = g * 2 + zp
    yc, h = lax.rem(y, 4), y // 4

    def place(px, pz, pc, py):
        return ((px * NZ + pz) * NC + pc, py)

    y_peers = [place(x, z, c, lax.rem(y + d, NY)) for d in RING8]
    y4_peers = [place(x, z, c, lax.rem(y + d, NY)) for d in (2, 1, 7)]
    z_peers = [place(x, lax.rem(z + d, NZ), c, y) for d in RING8]
    z4_peers = [place(x, lax.rem(z + d, NZ), c, y) for d in (4, 2, 6)]
    g_pos = [(lax.rem(x + dx, NX), lax.rem(c + dc, NC)) for dx, dc in PLANE]
    g_peers = [place(px, z, pc, y) for px, pc in g_pos]
    z_pair = z + 1 - 2 * zp
    far_pos = [(lax.rem(x + dx, NX), lax.rem(c + dc, NC)) for dx in (2, 1, 3, 0) for dc in (1, 0)]
    r_peers, r_index = [], []
    for dx in (2, 1, 3, 0):
        for pair in (True, False):
            for dc in (1, 0):
                if dx == 0 and dc == 0 and not pair:
                    continue
                px, pc = lax.rem(x + dx, NX), lax.rem(c + dc, NC)
                r_peers.append(place(px, z_pair if pair else z, pc, y))
                r_index.append((px * NC + pc) * 2 + ((1 - zp) if pair else zp))

    loads = [
        pltpu.make_async_copy(a, b, isem.at[i])
        for i, (a, b) in enumerate(
            ((src_hbm, src_ref), (tgt_hbm, tgt_ref), (ls_hbm, ls_ref), (lt_hbm, lt_ref))
        )
    ]
    barrier = pltpu.get_barrier_semaphore()
    greeted = y_peers + z_peers + g_peers + [place(px, z_pair, pc, y) for px, pc in far_pos[:-1]]
    for peer in greeted:
        pl.semaphore_signal(barrier, inc=1, device_id=peer, device_id_type=MESH)

    for load in loads:
        load.start()

    def send(name, source, target, peer):
        i = IDX[name]
        pltpu.make_async_remote_copy(
            src_ref=source, dst_ref=target, send_sem=ssem.at[i], recv_sem=rsem.at[i],
            device_id=peer, device_id_type=MESH,
        ).start()

    def share(name, buf, me, peers, value):
        buf[me] = value
        for peer in peers:
            send(name, buf.at[me], buf.at[me], peer)

    def settle(sems, name, buf, n):
        span = buf.at[pl.ds(0, n)]
        pltpu.make_async_copy(span, span, sems.at[IDX[name]]).wait()

    for load in loads:
        load.wait()
    src_t, tgt_t = src_ref[...].astype(F32), tgt_ref[...].astype(F32)
    src_own, tgt_own = with_norms_s(src_t), with_norms_t(tgt_t)
    scores = tn(tgt_own, src_own) * (-SCALE)
    highest = jnp.max(scores, axis=0, keepdims=True)
    partial = highest + jnp.log2(jnp.sum(jnp.exp2(scores - highest), axis=0, keepdims=True))

    pl.semaphore_wait(barrier, len(greeted))
    share("y1", y1, y, y_peers, partial)
    share("src", src_all, zi, z4_peers, src_t)
    tgt_all[0, y] = tgt_t[: D // 2]
    tgt_all[1, y] = tgt_t[D // 2 :]
    mt_own[...] = scores

    log_a = ls_ref[...] * LOG2E
    lanes_of = (iota((8, T), 1) % 8 == iota((8, T), 0)).astype(F32)
    spread = (iota((T, 128), 0) // 8 == iota((T, 128), 1)).astype(F32)
    log_b_own = lax.dot_general(
        lt_ref[...] * LOG2E * lanes_of, spread, (((1,), (0,)), ((), ())),
        preferred_element_type=F32, precision=lax.Precision.HIGHEST,
    )
    lane = iota((8, 128), 1)

    settle(rsem, "y1", y1, 7)
    for peer in y_peers[:3]:
        send("tgt", tgt_all.at[c, y], tgt_all.at[c, y], peer)
    f_own = log_a - lse2(y1[...])

    packed = jnp.zeros((8, 128), F32)
    for k in range(NK):
        s = mt_own[8 * k : 8 * k + 8, :] + f_own
        highest = jnp.max(s, axis=1, keepdims=True)
        total = jnp.sum(jnp.exp2(s - highest), axis=1, keepdims=True)
        packed = jnp.where(lane == k, highest + jnp.log2(total), packed)
    share("p1", p1, g, g_peers, packed)
    share("fa", fa, zi, z4_peers, jnp.concatenate([f_own, log_a], axis=1))
    settle(rsem, "p1", p1, 7)
    share("z1", z1, z, z_peers, lse2(p1[...]))

    settle(rsem, "src", src_all, 3)
    settle(rsem, "fa", fa, 3)
    mass_a = jnp.exp2(fa[:, :, S:])

    def fill(half, points):
        for zz in range(ZH):
            inner = tn(points, with_norms_s(src_all[zz]))
            k_ref[half, zz] = inner * (-SCALE) + (fa[zz][:, :S] + SHIFT)

    fill(h, tgt_own)
    sibling = place(x, z, 1 - c, y)

    def forward(arrived, name, distances):
        settle(rsem, arrived, tgt_all.at[0], len(distances))
        for d in distances:
            other = lax.rem(y + d, NY)
            send(name, tgt_all.at[c, other], tgt_all.at[c, other], sibling)

    def build(half, potential, acc):
        for k in range(NK):
            block = jnp.exp2(k_ref[half, :, 8 * k : 8 * k + 8, :] + potential[:, k : k + 1])
            k_ref[half, :, 8 * k : 8 * k + 8, :] = block
            if acc is not None:
                acc = acc + block
        return acc

    def row_pass(v):
        acc = jnp.zeros((ZH, 8, S), F32)
        for half in range(YH):
            for k in range(NK):
                n = half * NK + k
                acc = acc + k_ref[half, :, 8 * k : 8 * k + 8, :] * v[:, n : n + 1]
        return jnp.sum(acc, axis=1, keepdims=True)

    def col_half(half, u, first, out):
        ub = jnp.broadcast_to(u, (ZH, 8, S))
        for k in range(NK):
            block = k_ref[half, :, 8 * k : 8 * k + 8, :] * ub
            t = jnp.sum(block, axis=0)
            t = t[:, :128] + t[:, 128:]
            out = jnp.where(lane == first + k, jnp.sum(t, axis=1, keepdims=True), out)
        return out

    def col_pass(u):
        return col_half(1, u, NK, col_half(0, u, 0, jnp.zeros((8, 128), F32)))

    settle(rsem, "z1", z1, 7)
    g1_own = log_b_own - lse2(z1[...])
    ga[0] = jnp.concatenate([g1_own, log_b_own], axis=0)
    send("ga", ga.at[0], ga.at[1], place(x, z, c, lax.rem(y + 4, NY)))
    acc = build(h, g1_own, jnp.zeros((ZH, 8, S), F32))
    share("y2", y2, y, y_peers, jnp.sum(acc, axis=1, keepdims=True))
    forward("tgt", "fwd", RING8[:3])
    settle(rsem, "fwd", tgt_all.at[0], 3)

    def full(yy, carry):
        block = jnp.concatenate([tgt_all[0, yy], tgt_all[1, yy]], axis=0)
        mf[yy] = tn(with_norms_t(block), src_own) * (-SCALE)
        return carry

    other = lax.rem(y + 4, NY)
    fill(1 - h, with_norms_t(jnp.concatenate([tgt_all[0, other], tgt_all[1, other]], axis=0)))
    settle(rsem, "ga", ga, 1)
    g1_far, log_b_far = ga[1][:8], ga[1][8:]

    def both_halves(own, far):
        own, far = own[:, :NK], far[:, :NK]
        return jnp.where(h == 0, jnp.concatenate([own, far], axis=1), jnp.concatenate([far, own], axis=1))

    g1 = both_halves(g1_own, g1_far)
    mass_b = jnp.exp2(both_halves(log_b_own, log_b_far))
    build(1 - h, g1_far, None)

    settle(rsem, "y2", y2, 7)
    for peer in y_peers[3:]:
        send("tgb", tgt_all.at[c, y], tgt_all.at[c, y], peer)
    u = mass_a / jnp.sum(y2[...], axis=0)
    share("p2", p2, m, r_peers, col_pass(u))
    settle(rsem, "p2", p2, NR - 1)
    v = mass_b / jnp.sum(p2[...], axis=0)

    share("y3", y3, yc, y4_peers, row_pass(v))
    settle(rsem, "y3", y3, 3)
    u = mass_a / jnp.sum(y3[...], axis=0)
    share("p3", p3, m, r_peers, col_pass(u))
    forward("tgb", "fwb", RING8[3:])
    settle(rsem, "p3", p3, NR - 1)
    v = mass_b / jnp.sum(p3[...], axis=0)

    share("y4", y4, yc, y4_peers, row_pass(v))
    settle(rsem, "fwb", tgt_all.at[0], 4)
    lax.fori_loop(0, NY, full, 0)
    for zz in range(ZH):
        wb[:, zz * S : (zz + 1) * S] = k_ref[h, zz].astype(BF16)
    settle(rsem, "y4", y4, 3)
    sums = jnp.sum(y4[...], axis=0)
    u = mass_a / sums
    for zz in range(ZH):
        mass = jnp.broadcast_to(u[zz], (16, S))
        scaled = jnp.concatenate([src_all[zz] * u[zz], mass], axis=0)
        high = scaled.astype(BF16)
        low = (scaled - high.astype(F32)).astype(BF16)
        ste[:, zz * S : (zz + 1) * S] = jnp.concatenate([high, low], axis=0)
    weighted = nt(ste[...], wb[...])
    weighted = weighted[: D + 16] + weighted[D + 16 :]
    for n in range(NR):
        numt[n] = weighted[n * FR : n * FR + FR]
    num[m] = numt[m]
    for peer, index in zip(r_peers, r_index):
        send("num", numt.at[index], num.at[m], peer)
    share("p4", p4, m, r_peers, col_pass(u))
    share("den", den, m, r_peers, weighted[D : D + 1])

    f_last = f_own + log_a - jnp.log2(jnp.sum(y4[:, zi], axis=0)) + SHIFT

    def add_f(yy, carry):
        mf[yy] = mf[yy] + f_last
        return carry

    lax.fori_loop(0, NY, add_f, 0)
    settle(rsem, "num", num, NR - 1)
    share("map", mapped, m, r_peers, jnp.sum(num[...], axis=0))
    settle(rsem, "p4", p4, NR - 1)
    g4 = g1 + jnp.log2(mass_b / jnp.sum(p4[...], axis=0))
    yg[yc] = g4
    for i, peer in enumerate(y4_peers):
        pltpu.make_async_remote_copy(
            src_ref=yg.at[yc], dst_ref=yg.at[yc], send_sem=gsem.at[i], recv_sem=gsem.at[3 + i],
            device_id=peer, device_id_type=MESH,
        ).start()

    def finish(cls):
        potential = yg[cls]
        acc = jnp.zeros((2 * D, S), F32)
        for half in range(YH):
            yy = cls + 4 * half
            parts = []
            for k in range(NK):
                n = half * NK + k
                parts.append(jnp.exp2(mf[yy, 8 * k : 8 * k + 8, :] + potential[:, n : n + 1]))
            weight = jnp.concatenate(parts, axis=0).astype(BF16)
            block = jnp.concatenate([tgt_all[0, yy], tgt_all[1, yy], jnp.ones((D, T), F32)], axis=0)
            acc = acc + nn(block.astype(BF16), weight)
        both[cls] = acc

    finish(yc)
    for i, d in ((2, 1), (1, 7), (0, 6)):
        cls = lax.rem(y + d, 4)
        pltpu.make_async_copy(yg.at[cls], yg.at[cls], gsem.at[3 + i]).wait()
        finish(cls)
    maps = jnp.sum(both[...], axis=0)
    out_s[...] = maps[:D] / maps[D:]

    settle(rsem, "den", den, NR - 1)
    total = jnp.sum(den[...], axis=0)
    settle(rsem, "map", mapped, NR - 1)
    for n in range(NR):
        out_t[n * FR : n * FR + FR, :] = mapped[n] / total

    for name, buf, n in (
        ("y1", y1, 7), ("y2", y2, 7), ("y3", y3, 3), ("y4", y4, 3), ("p1", p1, 7), ("z1", z1, 7),
        ("p2", p2, NR - 1), ("p3", p3, NR - 1), ("p4", p4, NR - 1), ("den", den, NR - 1), ("num", num, NR - 1),
        ("map", mapped, NR - 1), ("src", src_all, 3), ("fa", fa, 3), ("ga", ga, 1),
        ("tgt", tgt_all.at[0], 3), ("fwd", tgt_all.at[0], 3), ("tgb", tgt_all.at[0], 4), ("fwb", tgt_all.at[0], 4),
    ):
        settle(ssem, name, buf, n)
    for i in range(3):
        pltpu.make_async_copy(yg.at[0], yg.at[0], gsem.at[i]).wait()


def deliver(s_in, t_in, s_out, t_out, sems):
    copies = [
        pltpu.make_async_copy(s_in, s_out, sems.at[0]),
        pltpu.make_async_copy(t_in, t_out, sems.at[1]),
    ]
    for copy in copies:
        copy.start()
    for copy in copies:
        copy.wait()


def per_device(source, target, log_source, log_target):
    vmem = pl.BlockSpec(memory_space=pltpu.VMEM)
    n = len(PHASES)
    scratch = [
        pltpu.VMEM((NY, 1, S), F32),
        pltpu.VMEM((NY, ZH, 1, S), F32),
        pltpu.VMEM((4, ZH, 1, S), F32),
        pltpu.VMEM((4, ZH, 1, S), F32),
        pltpu.VMEM((4, 8, 128), F32),
        pltpu.VMEM((NG, 8, 128), F32),
        pltpu.VMEM((NZ, 8, 128), F32),
        pltpu.VMEM((NR, 8, 128), F32),
        pltpu.VMEM((NR, 8, 128), F32),
        pltpu.VMEM((NR, 8, 128), F32),
        pltpu.VMEM((NR, 1, T), F32),
        pltpu.VMEM((NR, FR, T), F32),
        pltpu.VMEM((NR, FR, T), F32),
        pltpu.VMEM((ZH, D, S), F32),
        pltpu.VMEM((ZH, 1, 2 * S), F32),
        pltpu.VMEM((2, 16, 128), F32),
        pltpu.VMEM((2, NY, D // 2, T), F32),
        pltpu.VMEM((NR, FR, T), F32),
        pltpu.VMEM((T, S), F32),
        pltpu.VMEM((YH, ZH, T, S), F32),
        pltpu.VMEM((NY, T, S), F32),
        pltpu.VMEM((T, ZH * S), BF16),
        pltpu.VMEM((2 * (D + 16), ZH * S), BF16),
        pltpu.VMEM((D, S), BF16),
        pltpu.VMEM((D, T), BF16),
        pltpu.VMEM((1, S), F32),
        pltpu.VMEM((1, T), F32),
        pltpu.VMEM((4, 2 * D, S), F32),
        pltpu.SemaphoreType.DMA((n,)),
        pltpu.SemaphoreType.DMA((n,)),
        pltpu.SemaphoreType.DMA((4,)),
        pltpu.SemaphoreType.DMA((6,)),
    ]
    source_map, target_map = pl.pallas_call(
        kernel,
        out_shape=(pltpu.VMEM((D, S), F32), pltpu.VMEM((D, T), F32)),
        in_specs=[pl.BlockSpec(memory_space=pltpu.HBM)] * 4,
        out_specs=(vmem, vmem),
        scratch_shapes=scratch,
        compiler_params=pltpu.CompilerParams(
            collective_id=0, has_side_effects=True, vmem_limit_bytes=62 * 1024 * 1024
        ),
    )(source.T, target.T, log_source.reshape(1, S), log_target.reshape(1, T))
    source_map, target_map = pl.pallas_call(
        deliver,
        out_shape=(jax.ShapeDtypeStruct((D, S), F32), jax.ShapeDtypeStruct((D, T), F32)),
        in_specs=[pl.BlockSpec(memory_space=pltpu.VMEM)] * 2,
        out_specs=(pl.BlockSpec(memory_space=pl.ANY),) * 2,
        scratch_shapes=[pltpu.SemaphoreType.DMA((2,))],
        compiler_params=pltpu.CompilerParams(vmem_limit_bytes=2 * 1024 * 1024),
    )(source_map, target_map)
    return source_map.T, target_map.T


def solution(mesh):
    in_specs = (P("row", None), P("col", None), P("row"), P("col"))
    out_specs = (P("row", None), P("col", None))
    return jax.shard_map(
        per_device, mesh=mesh, in_specs=in_specs, out_specs=out_specs, check_vma=False
    )
```

```python
import jax
import jax.numpy as jnp
from jax import lax
from jax.experimental import pallas as pl
from jax.experimental.pallas import tpu as pltpu
from jax.sharding import PartitionSpec as P

EPS = 3.0
LOG2E = 1.4426950408889634
SCALE = LOG2E / EPS
SHIFT = 40.0

NX, NZ, NC, NY = 4, 8, 2, 8
NG = NX * NC
ZH, YH = 4, 2
NR = NG * 2
FR = 64 // NR
S, T, D = 256, 512, 64
NK = T // 8
F32, BF16 = jnp.float32, jnp.bfloat16
MESH = pl.DeviceIdType.MESH
RING8 = (4, 3, 5, 2, 6, 1, 7)
PLANE = tuple((dx, dc) for dx in (2, 1, 3) for dc in (1, 0)) + ((0, 1),)

PHASES = (
    "y1", "y2", "y3", "y4", "p1", "z1", "p2", "p3", "p4", "den", "num", "map", "src", "fa", "ga", "tgt", "fwd",
    "tgb", "fwb",
)
IDX = {name: i for i, name in enumerate(PHASES)}


def iota(shape, dim):
    return lax.broadcasted_iota(jnp.int32, shape, dim)


def lse2(slots):
    highest = jnp.max(slots, axis=0)
    return highest + jnp.log2(jnp.sum(jnp.exp2(slots - highest[None]), axis=0))


def nt(a, b):
    return lax.dot_general(a, b, (((1,), (1,)), ((), ())), preferred_element_type=F32)


def nn(a, b):
    return lax.dot_general(a, b, (((1,), (0,)), ((), ())), preferred_element_type=F32)


def tn(a, b):
    return lax.dot_general(a, b, (((0,), (0,)), ((), ())), preferred_element_type=F32)


def norm_rows(points):
    norm = jnp.sum(points * points, axis=0, keepdims=True)
    first = norm.astype(BF16).astype(F32)
    second = (norm - first).astype(BF16).astype(F32)
    third = norm - first - second
    shape = (8, points.shape[1])
    row = iota(shape, 0)
    return jnp.where(row == 0, first, jnp.where(row == 1, second, jnp.where(row == 2, third, 0.0)))


def with_norms_s(points):
    ones = jnp.ones((8, points.shape[1]), F32)
    return jnp.concatenate([points, ones, norm_rows(points)], axis=0).astype(BF16)


def with_norms_t(points):
    ones = jnp.ones((8, points.shape[1]), F32)
    return jnp.concatenate([points * -2.0, norm_rows(points), ones], axis=0).astype(BF16)


def kernel(
    src_hbm, tgt_hbm, ls_hbm, lt_hbm, out_s, out_t,
    y1, y2, y3, y4, yg, p1, z1, p2, p3, p4, den, num, mapped, src_all, fa, ga, tgt_all,
    numt, mt_own, k_ref, mf, wb, ste, src_ref, tgt_ref, ls_ref, lt_ref, both, ssem, rsem, isem, gsem,
):
    row, y = lax.axis_index("row"), lax.axis_index("col")
    x, z, c = row // (NZ * NC), lax.rem(row // NC, NZ), lax.rem(row, NC)
    g = x * NC + c
    zp, zi = lax.rem(z, 2), z // 2
    m = g * 2 + zp
    yc, h = lax.rem(y, 4), y // 4

    def place(px, pz, pc, py):
        return ((px * NZ + pz) * NC + pc, py)

    y_peers = [place(x, z, c, lax.rem(y + d, NY)) for d in RING8]
    y4_peers = [place(x, z, c, lax.rem(y + d, NY)) for d in (2, 1, 7)]
    z_peers = [place(x, lax.rem(z + d, NZ), c, y) for d in RING8]
    z4_peers = [place(x, lax.rem(z + d, NZ), c, y) for d in (4, 2, 6)]
    g_pos = [(lax.rem(x + dx, NX), lax.rem(c + dc, NC)) for dx, dc in PLANE]
    g_peers = [place(px, z, pc, y) for px, pc in g_pos]
    z_pair = z + 1 - 2 * zp
    far_pos = [(lax.rem(x + dx, NX), lax.rem(c + dc, NC)) for dx in (2, 1, 3, 0) for dc in (1, 0)]
    r_peers, r_index = [], []
    for dx in (2, 1, 3, 0):
        for pair in (True, False):
            for dc in (1, 0):
                if dx == 0 and dc == 0 and not pair:
                    continue
                px, pc = lax.rem(x + dx, NX), lax.rem(c + dc, NC)
                r_peers.append(place(px, z_pair if pair else z, pc, y))
                r_index.append((px * NC + pc) * 2 + ((1 - zp) if pair else zp))

    loads = [
        pltpu.make_async_copy(a, b, isem.at[i])
        for i, (a, b) in enumerate(
            ((src_hbm, src_ref), (tgt_hbm, tgt_ref), (ls_hbm, ls_ref), (lt_hbm, lt_ref))
        )
    ]
    barrier = pltpu.get_barrier_semaphore()
    greeted = y_peers + z_peers + g_peers + [place(px, z_pair, pc, y) for px, pc in far_pos[:-1]]
    for peer in greeted:
        pl.semaphore_signal(barrier, inc=1, device_id=peer, device_id_type=MESH)

    for load in loads:
        load.start()

    def send(name, source, target, peer):
        i = IDX[name]
        pltpu.make_async_remote_copy(
            src_ref=source, dst_ref=target, send_sem=ssem.at[i], recv_sem=rsem.at[i],
            device_id=peer, device_id_type=MESH,
        ).start()

    def share(name, buf, me, peers, value):
        buf[me] = value
        for peer in peers:
            send(name, buf.at[me], buf.at[me], peer)

    def settle(sems, name, buf, n):
        span = buf.at[pl.ds(0, n)]
        pltpu.make_async_copy(span, span, sems.at[IDX[name]]).wait()

    for load in loads:
        load.wait()
    src_t, tgt_t = src_ref[...].astype(F32), tgt_ref[...].astype(F32)
    src_own, tgt_own = with_norms_s(src_t), with_norms_t(tgt_t)
    scores = tn(tgt_own, src_own) * (-SCALE)
    highest = jnp.max(scores, axis=0, keepdims=True)
    partial = highest + jnp.log2(jnp.sum(jnp.exp2(scores - highest), axis=0, keepdims=True))

    pl.semaphore_wait(barrier, len(greeted))
    share("y1", y1, y, y_peers, partial)
    share("src", src_all, zi, z4_peers, src_t)
    tgt_all[0, y] = tgt_t[: D // 2]
    tgt_all[1, y] = tgt_t[D // 2 :]
    mt_own[...] = scores

    log_a = ls_ref[...] * LOG2E
    lanes_of = (iota((8, T), 1) % 8 == iota((8, T), 0)).astype(F32)
    spread = (iota((T, 128), 0) // 8 == iota((T, 128), 1)).astype(F32)
    log_b_own = lax.dot_general(
        lt_ref[...] * LOG2E * lanes_of, spread, (((1,), (0,)), ((), ())),
        preferred_element_type=F32, precision=lax.Precision.HIGHEST,
    )
    lane = iota((8, 128), 1)

    settle(rsem, "y1", y1, 7)
    for peer in y_peers[:3]:
        send("tgt", tgt_all.at[c, y], tgt_all.at[c, y], peer)
    f_own = log_a - lse2(y1[...])

    packed = jnp.zeros((8, 128), F32)
    for k in range(NK):
        s = mt_own[8 * k : 8 * k + 8, :] + f_own
        highest = jnp.max(s, axis=1, keepdims=True)
        total = jnp.sum(jnp.exp2(s - highest), axis=1, keepdims=True)
        packed = jnp.where(lane == k, highest + jnp.log2(total), packed)
    share("p1", p1, g, g_peers, packed)
    share("fa", fa, zi, z4_peers, jnp.concatenate([f_own, log_a], axis=1))
    settle(rsem, "p1", p1, 7)
    share("z1", z1, z, z_peers, lse2(p1[...]))

    settle(rsem, "src", src_all, 3)
    settle(rsem, "fa", fa, 3)
    mass_a = jnp.exp2(fa[:, :, S:])

    def fill(half, points):
        for zz in range(ZH):
            inner = tn(points, with_norms_s(src_all[zz]))
            k_ref[half, zz] = inner * (-SCALE) + (fa[zz][:, :S] + SHIFT)

    fill(h, tgt_own)
    sibling = place(x, z, 1 - c, y)

    def forward(arrived, name, distances):
        settle(rsem, arrived, tgt_all.at[0], len(distances))
        for d in distances:
            other = lax.rem(y + d, NY)
            send(name, tgt_all.at[c, other], tgt_all.at[c, other], sibling)

    def build(half, potential, acc):
        for k in range(NK):
            block = jnp.exp2(k_ref[half, :, 8 * k : 8 * k + 8, :] + potential[:, k : k + 1])
            k_ref[half, :, 8 * k : 8 * k + 8, :] = block
            if acc is not None:
                acc = acc + block
        return acc

    def row_pass(v):
        acc = jnp.zeros((ZH, 8, S), F32)
        for half in range(YH):
            for k in range(NK):
                n = half * NK + k
                acc = acc + k_ref[half, :, 8 * k : 8 * k + 8, :] * v[:, n : n + 1]
        return jnp.sum(acc, axis=1, keepdims=True)

    def col_half(half, u, first, out):
        ub = jnp.broadcast_to(u, (ZH, 8, S))
        for k in range(NK):
            block = k_ref[half, :, 8 * k : 8 * k + 8, :] * ub
            t = jnp.sum(block, axis=0)
            t = t[:, :128] + t[:, 128:]
            out = jnp.where(lane == first + k, jnp.sum(t, axis=1, keepdims=True), out)
        return out

    def col_pass(u):
        return col_half(1, u, NK, col_half(0, u, 0, jnp.zeros((8, 128), F32)))

    settle(rsem, "z1", z1, 7)
    g1_own = log_b_own - lse2(z1[...])
    ga[0] = jnp.concatenate([g1_own, log_b_own], axis=0)
    send("ga", ga.at[0], ga.at[1], place(x, z, c, lax.rem(y + 4, NY)))
    acc = build(h, g1_own, jnp.zeros((ZH, 8, S), F32))
    share("y2", y2, y, y_peers, jnp.sum(acc, axis=1, keepdims=True))
    forward("tgt", "fwd", RING8[:3])
    settle(rsem, "fwd", tgt_all.at[0], 3)

    def full(yy, carry):
        block = jnp.concatenate([tgt_all[0, yy], tgt_all[1, yy]], axis=0)
        mf[yy] = tn(with_norms_t(block), src_own) * (-SCALE)
        return carry

    other = lax.rem(y + 4, NY)
    fill(1 - h, with_norms_t(jnp.concatenate([tgt_all[0, other], tgt_all[1, other]], axis=0)))
    settle(rsem, "ga", ga, 1)
    g1_far, log_b_far = ga[1][:8], ga[1][8:]

    def both_halves(own, far):
        own, far = own[:, :NK], far[:, :NK]
        return jnp.where(h == 0, jnp.concatenate([own, far], axis=1), jnp.concatenate([far, own], axis=1))

    g1 = both_halves(g1_own, g1_far)
    mass_b = jnp.exp2(both_halves(log_b_own, log_b_far))
    build(1 - h, g1_far, None)

    settle(rsem, "y2", y2, 7)
    for peer in y_peers[3:]:
        send("tgb", tgt_all.at[c, y], tgt_all.at[c, y], peer)
    u = mass_a / jnp.sum(y2[...], axis=0)
    share("p2", p2, m, r_peers, col_pass(u))
    settle(rsem, "p2", p2, NR - 1)
    v = mass_b / jnp.sum(p2[...], axis=0)

    share("y3", y3, yc, y4_peers, row_pass(v))
    settle(rsem, "y3", y3, 3)
    u = mass_a / jnp.sum(y3[...], axis=0)
    share("p3", p3, m, r_peers, col_pass(u))
    forward("tgb", "fwb", RING8[3:])
    settle(rsem, "p3", p3, NR - 1)
    v = mass_b / jnp.sum(p3[...], axis=0)

    share("y4", y4, yc, y4_peers, row_pass(v))
    settle(rsem, "fwb", tgt_all.at[0], 4)
    lax.fori_loop(0, NY, full, 0)
    for zz in range(ZH):
        wb[:, zz * S : (zz + 1) * S] = k_ref[h, zz].astype(BF16)
    settle(rsem, "y4", y4, 3)
    sums = jnp.sum(y4[...], axis=0)
    u = mass_a / sums
    share("p4", p4, m, r_peers, col_pass(u))
    for zz in range(ZH):
        mass = jnp.broadcast_to(u[zz], (16, S))
        scaled = jnp.concatenate([src_all[zz] * u[zz], mass], axis=0)
        high = scaled.astype(BF16)
        low = (scaled - high.astype(F32)).astype(BF16)
        ste[:, zz * S : (zz + 1) * S] = jnp.concatenate([high, low], axis=0)
    weighted = nt(ste[...], wb[...])
    weighted = weighted[: D + 16] + weighted[D + 16 :]
    for n in range(NR):
        numt[n] = weighted[n * FR : n * FR + FR]
    num[m] = numt[m]
    for peer, index in zip(r_peers, r_index):
        send("num", numt.at[index], num.at[m], peer)
    share("den", den, m, r_peers, weighted[D : D + 1])

    f_last = f_own + log_a - jnp.log2(jnp.sum(y4[:, zi], axis=0)) + SHIFT

    def add_f(yy, carry):
        mf[yy] = mf[yy] + f_last
        return carry

    lax.fori_loop(0, NY, add_f, 0)
    settle(rsem, "num", num, NR - 1)
    share("map", mapped, m, r_peers, jnp.sum(num[...], axis=0))
    settle(rsem, "p4", p4, NR - 1)
    g4 = g1 + jnp.log2(mass_b / jnp.sum(p4[...], axis=0))
    yg[yc] = g4
    for i, peer in enumerate(y4_peers):
        pltpu.make_async_remote_copy(
            src_ref=yg.at[yc], dst_ref=yg.at[yc], send_sem=gsem.at[i], recv_sem=gsem.at[3 + i],
            device_id=peer, device_id_type=MESH,
        ).start()

    def finish(cls):
        potential = yg[cls]
        acc = jnp.zeros((2 * D, S), F32)
        for half in range(YH):
            yy = cls + 4 * half
            parts = []
            for k in range(NK):
                n = half * NK + k
                parts.append(jnp.exp2(mf[yy, 8 * k : 8 * k + 8, :] + potential[:, n : n + 1]))
            weight = jnp.concatenate(parts, axis=0).astype(BF16)
            block = jnp.concatenate([tgt_all[0, yy], tgt_all[1, yy], jnp.ones((D, T), F32)], axis=0)
            acc = acc + nn(block.astype(BF16), weight)
        both[cls] = acc

    finish(yc)
    for i, d in ((2, 1), (1, 7), (0, 6)):
        cls = lax.rem(y + d, 4)
        pltpu.make_async_copy(yg.at[cls], yg.at[cls], gsem.at[3 + i]).wait()
        finish(cls)
    maps = jnp.sum(both[...], axis=0)
    out_s[...] = maps[:D] / maps[D:]

    settle(rsem, "den", den, NR - 1)
    total = jnp.sum(den[...], axis=0)
    settle(rsem, "map", mapped, NR - 1)
    for n in range(NR):
        out_t[n * FR : n * FR + FR, :] = mapped[n] / total

    for name, buf, n in (
        ("y1", y1, 7), ("y2", y2, 7), ("y3", y3, 3), ("y4", y4, 3), ("p1", p1, 7), ("z1", z1, 7),
        ("p2", p2, NR - 1), ("p3", p3, NR - 1), ("p4", p4, NR - 1), ("den", den, NR - 1), ("num", num, NR - 1),
        ("map", mapped, NR - 1), ("src", src_all, 3), ("fa", fa, 3), ("ga", ga, 1),
        ("tgt", tgt_all.at[0], 3), ("fwd", tgt_all.at[0], 3), ("tgb", tgt_all.at[0], 4), ("fwb", tgt_all.at[0], 4),
    ):
        settle(ssem, name, buf, n)
    for i in range(3):
        pltpu.make_async_copy(yg.at[0], yg.at[0], gsem.at[i]).wait()


def deliver(s_in, t_in, s_out, t_out, sems):
    copies = [
        pltpu.make_async_copy(s_in, s_out, sems.at[0]),
        pltpu.make_async_copy(t_in, t_out, sems.at[1]),
    ]
    for copy in copies:
        copy.start()
    for copy in copies:
        copy.wait()


def per_device(source, target, log_source, log_target):
    vmem = pl.BlockSpec(memory_space=pltpu.VMEM)
    n = len(PHASES)
    scratch = [
        pltpu.VMEM((NY, 1, S), F32),
        pltpu.VMEM((NY, ZH, 1, S), F32),
        pltpu.VMEM((4, ZH, 1, S), F32),
        pltpu.VMEM((4, ZH, 1, S), F32),
        pltpu.VMEM((4, 8, 128), F32),
        pltpu.VMEM((NG, 8, 128), F32),
        pltpu.VMEM((NZ, 8, 128), F32),
        pltpu.VMEM((NR, 8, 128), F32),
        pltpu.VMEM((NR, 8, 128), F32),
        pltpu.VMEM((NR, 8, 128), F32),
        pltpu.VMEM((NR, 1, T), F32),
        pltpu.VMEM((NR, FR, T), F32),
        pltpu.VMEM((NR, FR, T), F32),
        pltpu.VMEM((ZH, D, S), F32),
        pltpu.VMEM((ZH, 1, 2 * S), F32),
        pltpu.VMEM((2, 16, 128), F32),
        pltpu.VMEM((2, NY, D // 2, T), F32),
        pltpu.VMEM((NR, FR, T), F32),
        pltpu.VMEM((T, S), F32),
        pltpu.VMEM((YH, ZH, T, S), F32),
        pltpu.VMEM((NY, T, S), F32),
        pltpu.VMEM((T, ZH * S), BF16),
        pltpu.VMEM((2 * (D + 16), ZH * S), BF16),
        pltpu.VMEM((D, S), BF16),
        pltpu.VMEM((D, T), BF16),
        pltpu.VMEM((1, S), F32),
        pltpu.VMEM((1, T), F32),
        pltpu.VMEM((4, 2 * D, S), F32),
        pltpu.SemaphoreType.DMA((n,)),
        pltpu.SemaphoreType.DMA((n,)),
        pltpu.SemaphoreType.DMA((4,)),
        pltpu.SemaphoreType.DMA((6,)),
    ]
    source_map, target_map = pl.pallas_call(
        kernel,
        out_shape=(pltpu.VMEM((D, S), F32), pltpu.VMEM((D, T), F32)),
        in_specs=[pl.BlockSpec(memory_space=pltpu.HBM)] * 4,
        out_specs=(vmem, vmem),
        scratch_shapes=scratch,
        compiler_params=pltpu.CompilerParams(
            collective_id=0, has_side_effects=True, vmem_limit_bytes=62 * 1024 * 1024
        ),
    )(source.T, target.T, log_source.reshape(1, S), log_target.reshape(1, T))
    source_map, target_map = pl.pallas_call(
        deliver,
        out_shape=(jax.ShapeDtypeStruct((D, S), F32), jax.ShapeDtypeStruct((D, T), F32)),
        in_specs=[pl.BlockSpec(memory_space=pltpu.VMEM)] * 2,
        out_specs=(pl.BlockSpec(memory_space=pl.ANY),) * 2,
        scratch_shapes=[pltpu.SemaphoreType.DMA((2,))],
        compiler_params=pltpu.CompilerParams(vmem_limit_bytes=2 * 1024 * 1024),
    )(source_map, target_map)
    return source_map.T, target_map.T


def solution(mesh):
    in_specs = (P("row", None), P("col", None), P("row"), P("col"))
    out_specs = (P("row", None), P("col", None))
    return jax.shard_map(
        per_device, mesh=mesh, in_specs=in_specs, out_specs=out_specs, check_vma=False
    )
```
